256 devices in a mesh: hour: 8 (over z), pair: 32 (over x, y, core).
Axes of the slice: x: 4, y: 4, z: 8, core: 2. Of those that a mesh axis runs over, the one named last changes fastest.
Arguments:
- raw_panels: bfloat16 [512, 24, 3, 3712], P('pair', 'hour'), may hold values from -6 to 6
- window_start: int32 [512, 24, 2], P('pair', 'hour'), may hold values from 0 to 2688
- valid_count: int32 [512, 24, 2], P('pair', 'hour'), may hold values from 512 to 1024
- send_rows: int32 [32, 32, 4], P('pair'), may hold values from 0 to 15, as said below
- pair_slots: int32 [2048, 2], P('pair'), may hold values from 0 to 127, as said below
Outputs:
- stacked: float32 [2048, 9, 256], P('pair')
The draws below stay inside these ranges and needn't reach their ends.
Inputs may be any that keep to these rules, and one draw needn't show every extreme that they name: `send_rows`: for each source and owner the 4 rows are different. `pair_slots`: the two slots of a pair differ; a slot s * 4 + c of owner q stands for the c-th row that source s sends to q.
All inputs are finite; a program needn't handle non-finite values.
Results may differ from the reference program's by a relative error of at most 0.0094.
Values may be sent and summed in bfloat16 or wider, within the bound.
No kernel may reach another device: no remote copies, remote signals or barrier semaphores. Data moves between devices by JAX's collectives and lax.ppermute only.
A program may use at most 64 MiB of HBM per device.

```python
import math
import jax
import jax.numpy as jnp
from jax import lax

NFFT = 1024
NFREQ = 512
LAGS = 256
RAW = 3712
WINDOWS = 2
HOURS = 24
STA_DEV = 16
STATIONS = 512
CAP = 4
PAIRS_DEV = 64
PAIRS = 2048
N_PAIR = 32


def draw_send_rows(key, part):
    keys = jax.random.split(key, N_PAIR * N_PAIR)
    chosen = jax.vmap(lambda single: jax.random.permutation(single, STA_DEV)[:CAP])(keys).astype(jnp.int32)
    spread = (jnp.arange(CAP, dtype=jnp.int32) * (STA_DEV - 1) // (CAP - 1)).astype(jnp.int32)
    chosen = chosen.at[0].set(spread)
    return chosen.reshape(N_PAIR, N_PAIR, CAP).astype(jnp.int32)


def draw_pair_slots(key, part):
    base_key = jax.random.fold_in(key, 11)
    key_count, key_first, key_second = jax.random.split(base_key, 3)
    counts = jax.random.randint(key_count, (N_PAIR, N_PAIR), 1, CAP + 1).astype(jnp.int32)
    diagonal = jnp.eye(N_PAIR, dtype=jnp.int32) > 0
    counts = jnp.where(diagonal, CAP, counts).astype(jnp.int32)
    totals = jnp.sum(counts, axis=0)
    ends = jnp.cumsum(counts, axis=0)
    begins = ends - counts
    first_pos = jax.random.randint(key_first, (N_PAIR, PAIRS_DEV), 0, 1 << 20) % totals[:, None]
    offsets = jax.random.randint(key_second, (N_PAIR, PAIRS_DEV), 0, 1 << 20) % (totals[:, None] - 1)
    second_pos = (first_pos + 1 + offsets) % totals[:, None]

    def to_slot(position):
        source = jnp.sum((ends.T[:, None, :] <= position[:, :, None]).astype(jnp.int32), axis=2)
        start_of = jnp.take_along_axis(begins.T, source, axis=1)
        return (source * CAP + position - start_of).astype(jnp.int32)
    slot_first = to_slot(first_pos)
    slot_second = to_slot(second_pos)
    owner_ids = jnp.arange(N_PAIR, dtype=jnp.int32)
    slot_first = slot_first.at[:, 0].set(owner_ids * CAP + CAP - 1)
    slot_second = slot_second.at[:, 0].set(owner_ids * CAP)
    slot_first = slot_first.at[:, 1].set(jnp.zeros((N_PAIR,), jnp.int32))
    slot_second = slot_second.at[:, 1].set(owner_ids * CAP + 1)
    return jnp.stack([slot_first, slot_second], axis=-1).reshape(PAIRS, 2).astype(jnp.int32)


def place_ends(values, rng, smallest, largest):
    extent = values.shape
    place = [jax.random.randint(jax.random.fold_in(rng, axis), (), 0, extent[axis]) for axis in range(len(extent))]
    values = values.at[tuple(place)].set(smallest)
    longest = extent.index(max(extent))
    place[longest] = (place[longest] + 1) % extent[longest]
    return values.at[tuple(place)].set(largest)


def steps_of(own_key, extent, cuts, smallest, largest):
    level, own = 1.0, jax.random.fold_in(own_key, 6)
    for dim, shards_of in cuts:
        steps = jnp.exp(jax.random.uniform(jax.random.fold_in(own, dim), (shards_of,), jnp.float32, smallest / len(cuts), largest / len(cuts)))
        level = level * jnp.repeat(steps, extent[dim] // shards_of).reshape([-1 if axis == dim else 1 for axis in range(len(extent))])
    return level


def centred(own_key, extent, scale, most, cuts=(), held_as=jnp.bfloat16):
    array = scale * jax.random.normal(own_key, extent, jnp.float32)
    if cuts:
        array = array * steps_of(own_key, extent, cuts, -0.22, 0.18)
    return jnp.clip(array, -most, most).astype(held_as)


def setup_inputs(seed: int = 0) -> dict:
    splits = jax.random.split(jax.random.key(seed), 6)
    return {
        "raw_panels": centred(splits[0], (STATIONS, HOURS, 3, RAW), 1.0, 6.0, ((0, 32), (1, 8))),
        "window_start": place_ends(jax.random.randint(splits[1], (STATIONS, HOURS, WINDOWS), 0, RAW - NFFT + 1), jax.random.fold_in(splits[1], 1), 0, RAW - NFFT).astype(jnp.int32),
        "valid_count": place_ends(jax.random.randint(splits[2], (STATIONS, HOURS, WINDOWS), NFFT // 2, NFFT + 1), jax.random.fold_in(splits[2], 1), NFFT // 2, NFFT).astype(jnp.int32),
        "send_rows": draw_send_rows(jax.random.fold_in(splits[5], 71), 0),
        "pair_slots": draw_pair_slots(jax.random.fold_in(splits[5], 71), 0),
    }


smooth_half = 11
eps_white = 1e-06

def make_dft(length, nfreq):
    time_index = lax.broadcasted_iota(jnp.int32, (length, nfreq), 0)
    freq_index = lax.broadcasted_iota(jnp.int32, (length, nfreq), 1)
    angles = (time_index * freq_index % length).astype(jnp.float32) * (2.0 * math.pi / length)
    return jnp.concatenate([jnp.cos(angles), -jnp.sin(angles)], axis=1).astype(jnp.bfloat16)

def make_band(nfreq):
    row_index = lax.broadcasted_iota(jnp.int32, (nfreq, nfreq), 0)
    col_index = lax.broadcasted_iota(jnp.int32, (nfreq, nfreq), 1)
    return (jnp.abs(row_index - col_index) <= smooth_half).astype(jnp.float32)

def make_lags(nfreq, length, lags):
    freq_index = lax.broadcasted_iota(jnp.int32, (nfreq, lags), 0)
    shift_lag = lax.broadcasted_iota(jnp.int32, (nfreq, lags), 1) - lags // 2
    angles = (freq_index * shift_lag % length).astype(jnp.float32) * (2.0 * math.pi / length)
    weights = jnp.where(freq_index == 0, 0.5, 1.0).astype(jnp.float32)
    return jnp.concatenate([weights * jnp.cos(angles), -weights * jnp.sin(angles)], axis=0).astype(jnp.bfloat16)

def cut_windows(panels, starts, counts, length):

    def take_one(panel, begin):
        return lax.dynamic_slice_in_dim(panel, begin, length, 1)
    pieces = jax.vmap(jax.vmap(take_one, in_axes=(None, 0)))(panels, starts)
    positions = lax.broadcasted_iota(jnp.int32, (1, 1, 1, length), 3)
    valid_mask = (positions < counts[:, :, None, None]).astype(jnp.float32)
    values = pieces.astype(jnp.float32) * valid_mask
    average = lax.optimization_barrier(jnp.sum(values, axis=3, keepdims=True)) / counts[:, :, None, None].astype(jnp.float32)
    return ((values - average) * valid_mask).astype(jnp.bfloat16)

def whiten(samples, dft_matrix, band_ones, nfreq):
    leading = samples.shape[:-1]
    spectrum = jnp.dot(samples.reshape(-1, samples.shape[-1]), dft_matrix, preferred_element_type=jnp.float32)
    spectrum = spectrum.reshape(leading + (2 * nfreq,))
    real_part = spectrum[..., :nfreq]
    imag_part = spectrum[..., nfreq:]
    amplitude = lax.optimization_barrier(jnp.sum(jnp.sqrt(real_part * real_part + imag_part * imag_part), axis=-2))
    smooth = jnp.dot(amplitude.reshape(-1, nfreq), band_ones, precision=lax.Precision.HIGHEST)
    smooth = smooth.reshape(amplitude.shape) / (3.0 * (2 * smooth_half + 1))
    divisor = jnp.concatenate([smooth, smooth], axis=-1) + eps_white
    return (spectrum / divisor[..., None, :]).astype(jnp.bfloat16)

def outer_sum(left_part, right_part):
    return lax.optimization_barrier(jnp.sum(left_part[:, :, :, None, :] * right_part[:, :, None, :, :], axis=1))

def hour_roots(spectra, first_index, second_index, lag_matrix, nfreq):
    pairs = first_index.shape[0]
    block_size = math.gcd(pairs, 256)
    windows = spectra.shape[1]
    lag_scale = 1.0 / math.sqrt(windows * nfreq)

    def one_block(indices):
        left_side = spectra[indices[0]].astype(jnp.float32)
        right_side = spectra[indices[1]].astype(jnp.float32)
        left_real, left_imag = (left_side[..., :nfreq], left_side[..., nfreq:])
        right_real, right_imag = (right_side[..., :nfreq], right_side[..., nfreq:])
        cross_real = outer_sum(left_real, right_real) + outer_sum(left_imag, right_imag)
        cross_imag = outer_sum(left_imag, right_real) - outer_sum(left_real, right_imag)
        cross = jnp.concatenate([cross_real, cross_imag], axis=-1).astype(jnp.bfloat16)
        lagged = jnp.dot(cross.reshape(-1, 2 * nfreq), lag_matrix, preferred_element_type=jnp.float32)
        lagged = lagged.reshape(block_size, 9, lag_matrix.shape[1]) * lag_scale
        return jnp.sign(lagged) * (jnp.sqrt(jnp.abs(lagged) + 0.01) - 0.1)
    blocks = (first_index.reshape(pairs // block_size, block_size), second_index.reshape(pairs // block_size, block_size))
    result = lax.map(one_block, blocks)
    return result.reshape(pairs, 9, lag_matrix.shape[1])

def finish(summed, hours_all):
    average = summed / hours_all
    return jnp.sign(average) * ((jnp.abs(average) + 0.1) * (jnp.abs(average) + 0.1) - 0.01)

def reference(raw_panels, window_start, valid_count, send_rows, pair_slots):
    owners = jnp.arange(PAIRS, dtype=jnp.int32) // PAIRS_DEV

    def station_of(slot):
        source = slot // CAP
        column = slot % CAP
        return (source * STA_DEV + send_rows[source, owners, column]).astype(jnp.int32)
    first_station = station_of(pair_slots[:, 0])
    second_station = station_of(pair_slots[:, 1])
    dft_matrix = make_dft(NFFT, NFREQ)
    band_ones = make_band(NFREQ)
    lag_matrix = make_lags(NFREQ, NFFT, LAGS)

    def hour_step(summed, hour):
        panels = lax.dynamic_index_in_dim(raw_panels, hour, 1, keepdims=False)
        starts = lax.dynamic_index_in_dim(window_start, hour, 1, keepdims=False)
        counts = lax.dynamic_index_in_dim(valid_count, hour, 1, keepdims=False)
        samples = cut_windows(panels, starts, counts, NFFT)
        spectra = whiten(samples, dft_matrix, band_ones, NFREQ)
        return (summed + hour_roots(spectra, first_station, second_station, lag_matrix, NFREQ), None)
    summed, _ = lax.scan(hour_step, jnp.zeros((PAIRS, 9, LAGS), jnp.float32), jnp.arange(HOURS, dtype=jnp.int32))
    return finish(summed, HOURS)
```

```python
import functools
import math

import jax
import jax.numpy as jnp
import ml_dtypes
import numpy as np
from jax import lax
from jax.experimental import pallas as pl
from jax.experimental.pallas import tpu as pltpu
from jax.sharding import PartitionSpec as P

NFFT = 1024
NFREQ = 512
LAGS = 256
COMPS = 3
WINDOWS = 2
PARTS = 2 * WINDOWS
SMOOTH_HALF = 11
EPS_WHITE = 1e-06
F32 = jnp.float32
BF16 = jnp.bfloat16


def dft_table():
    turns = np.outer(np.arange(NFFT), np.arange(NFREQ)) % NFFT
    angles = turns.astype(np.float32) * np.float32(2.0 * math.pi / NFFT)
    angles = angles.astype(np.float64)
    table = np.concatenate([np.cos(angles), -np.sin(angles)], axis=1)
    return table.astype(np.float32).astype(ml_dtypes.bfloat16)


def band_table():
    index = np.arange(NFREQ)
    band = np.abs(index[:, None] - index[None, :]) <= SMOOTH_HALF
    return band.astype(ml_dtypes.bfloat16)


def lag_table():
    turns = np.outer(np.arange(NFREQ), np.arange(LAGS) - LAGS // 2) % NFFT
    angles = turns.astype(np.float32) * np.float32(2.0 * math.pi / NFFT)
    angles = angles.astype(np.float64)
    weights = np.where(np.arange(NFREQ) == 0, 0.5, 1.0)[:, None]
    table = np.concatenate([weights * np.cos(angles), -weights * np.sin(angles)], axis=0)
    scale = 1.0 / math.sqrt(WINDOWS * NFREQ)
    return (table.astype(np.float32).astype(ml_dtypes.bfloat16) * scale).astype(ml_dtypes.bfloat16)


def column(row, size):
    here = lax.broadcasted_iota(jnp.int32, (size, size), 0)
    there = lax.broadcasted_iota(jnp.int32, (size, size), 1)
    spread = jnp.where(here == there, jnp.broadcast_to(row, (size, size)).astype(F32), 0.0)
    return jnp.sum(spread, axis=1, keepdims=True).astype(jnp.int32)


def cut(panel, start):
    raw = panel.shape[1]
    reach = raw - 2048
    bit = (start & 2048) != 0
    moved = jnp.where(bit, panel[:, 2048:], panel[:, :reach])
    samples = jnp.concatenate([moved, panel[:, reach : NFFT + 2048]], axis=1)
    for size in (1024, 512, 256, 128):
        bit = (start & size) != 0
        keep = NFFT + size
        samples = jnp.where(bit, samples[:, size : size + keep], samples[:, :keep])
    width = samples.shape[1]
    for size in (64, 32, 16, 8, 4, 2, 1):
        bit = (start & size) != 0
        samples = jnp.where(bit, pltpu.roll(samples, width - size, 1), samples)
    return samples[:, :NFFT]


def whiten_kernel(raw_ref, start_ref, count_ref, dft_ref, band_ref, pick_ref, out_ref, seg_ref, spec_ref, white_ref):
    stations = raw_ref.shape[2]
    time = lax.broadcasted_iota(jnp.int32, (stations, NFFT), 1)
    for w in range(WINDOWS):
        start = column(start_ref[0, w : w + 1, :], stations)
        count = column(count_ref[0, w : w + 1, :], stations)
        live = time < count
        share = count.astype(F32)
        for c in range(COMPS):
            piece = cut(raw_ref[0, c].astype(F32), start)
            piece = jnp.where(live, piece, 0.0)
            mean = jnp.sum(piece, axis=1, keepdims=True) / share
            row = (w * COMPS + c) * stations
            seg_ref[row : row + stations, :] = jnp.where(live, piece - mean, 0.0).astype(BF16)
    spec_ref[...] = jnp.dot(seg_ref[...], dft_ref[...], preferred_element_type=F32)
    amps = []
    for w in range(WINDOWS):
        total = jnp.zeros((stations, NFREQ), F32)
        for c in range(COMPS):
            row = (w * COMPS + c) * stations
            real = spec_ref[row : row + stations, :NFREQ]
            imag = spec_ref[row : row + stations, NFREQ:]
            total = total + jnp.sqrt(real * real + imag * imag)
        amps.append(total)
    amp = jnp.concatenate(amps, axis=0)
    rows = WINDOWS * stations
    high = amp.astype(BF16)
    rest = amp - high.astype(F32)
    middle = rest.astype(BF16)
    low = (rest - middle.astype(F32)).astype(BF16)
    sums = jnp.dot(jnp.concatenate([high, middle, low], axis=0), band_ref[...], preferred_element_type=F32)
    smooth = (sums[:rows] + sums[rows : 2 * rows] + sums[2 * rows :]) / (3.0 * (2 * SMOOTH_HALF + 1))
    inverse = 1.0 / (smooth + EPS_WHITE)
    for w in range(WINDOWS):
        factor = inverse[w * stations : (w + 1) * stations]
        for c in range(COMPS):
            row = (w * COMPS + c) * stations
            for r in range(2):
                part = spec_ref[row : row + stations, r * NFREQ : (r + 1) * NFREQ] * factor
                to = (2 * w + r) * stations
                white_ref[to : to + stations, c * NFREQ : (c + 1) * NFREQ] = part.astype(BF16)
    for c in range(COMPS):
        cols = slice(c * NFREQ, (c + 1) * NFREQ)
        picked = jnp.dot(pick_ref[...], white_ref[:, cols], preferred_element_type=F32).astype(BF16)
        out_ref[:, :, cols] = picked.reshape(out_ref.shape[0], out_ref.shape[1], NFREQ)


def correlate_kernel(recv_ref, pick_ref, lag_ref, out_ref, side_ref, cross_ref, total_ref):
    hour = pl.program_id(0)
    pairs = total_ref.shape[0] // (COMPS * COMPS)
    slots = recv_ref.shape[0] * recv_ref.shape[1]
    width = recv_ref.shape[2]
    for c in range(COMPS):
        cols = slice(c * NFREQ, (c + 1) * NFREQ)
        arrived = recv_ref[:, :, cols].reshape(slots, NFREQ)
        side_ref[:, cols] = jnp.dot(pick_ref[...], arrived, preferred_element_type=F32)

    for k in range(0, pairs, 16):
        for f in range(0, NFREQ, 128):
            def load(side, part, comp):
                row = (side * PARTS + part) * pairs + k
                col = comp * NFREQ + f
                return side_ref[row : row + 16, col : col + 128]
            left = [[load(0, part, comp) for comp in range(COMPS)] for part in range(PARTS)]
            right = [[load(1, part, comp) for comp in range(COMPS)] for part in range(PARTS)]
            for i in range(COMPS):
                for j in range(COMPS):
                    real = left[0][i] * right[0][j] + left[2][i] * right[2][j]
                    real = real + (left[1][i] * right[1][j] + left[3][i] * right[3][j])
                    imag = left[1][i] * right[0][j] + left[3][i] * right[2][j]
                    imag = imag - (left[0][i] * right[1][j] + left[2][i] * right[3][j])
                    row = (COMPS * i + j) * pairs + k
                    cross_ref[row : row + 16, f : f + 128] = real.astype(BF16)
                    cross_ref[row : row + 16, NFREQ + f : NFREQ + f + 128] = imag.astype(BF16)
    lagged = jnp.dot(cross_ref[...], lag_ref[...], preferred_element_type=F32)
    root = jnp.sqrt(jnp.abs(lagged) + 0.01) - 0.1
    root = jnp.where(lagged > 0.0, root, jnp.where(lagged < 0.0, -root, 0.0))

    @pl.when(hour == 0)
    def _():
        total_ref[...] = root

    @pl.when(hour > 0)
    def _():
        total_ref[...] += root

    @pl.when(hour == pl.num_programs(0) - 1)
    def _():
        out_ref[...] = total_ref[...].astype(BF16).reshape(out_ref.shape)


def whiten(panels, starts, counts, pick, owners, rows):
    hours, _, stations, raw = panels.shape
    width = COMPS * NFREQ
    whole = lambda shape: pl.BlockSpec(shape, lambda h: (0,) * len(shape))
    return pl.pallas_call(
        whiten_kernel,
        grid=(hours,),
        in_specs=[
            pl.BlockSpec((1, COMPS, stations, raw), lambda h: (h, 0, 0, 0)),
            pl.BlockSpec((1, WINDOWS, stations), lambda h: (h, 0, 0)),
            pl.BlockSpec((1, WINDOWS, stations), lambda h: (h, 0, 0)),
            whole((NFFT, 2 * NFREQ)),
            whole((NFREQ, NFREQ)),
            whole(pick.shape),
        ],
        out_specs=pl.BlockSpec((owners, rows, width), lambda h: (0, h, 0)),
        out_shape=jax.ShapeDtypeStruct((owners, hours * rows, width), BF16),
        scratch_shapes=[
            pltpu.VMEM((WINDOWS * COMPS * stations, NFFT), BF16),
            pltpu.VMEM((WINDOWS * COMPS * stations, 2 * NFREQ), F32),
            pltpu.VMEM((PARTS * stations, width), BF16),
        ],
        compiler_params=pltpu.CompilerParams(vmem_limit_bytes=40 * 2**20),
    )(panels, starts, counts, dft_table(), band_table(), pick)


def correlate(received, pick, pairs, rows, pieces):
    owners, all_rows, width = received.shape
    hours = all_rows // rows
    channels = COMPS * COMPS
    whole = lambda shape: pl.BlockSpec(shape, lambda h: (0,) * len(shape))
    piece = (pieces, channels * pairs // pieces, LAGS)
    return pl.pallas_call(
        correlate_kernel,
        grid=(hours,),
        in_specs=[
            pl.BlockSpec((owners, rows, width), lambda h: (0, h, 0)),
            whole(pick.shape),
            whole((2 * NFREQ, LAGS)),
        ],
        out_specs=whole(piece),
        out_shape=jax.ShapeDtypeStruct(piece, BF16),
        scratch_shapes=[
            pltpu.VMEM((2 * PARTS * pairs, width), F32),
            pltpu.VMEM((channels * pairs, 2 * NFREQ), BF16),
            pltpu.VMEM((channels * pairs, LAGS), F32),
        ],
        compiler_params=pltpu.CompilerParams(vmem_limit_bytes=40 * 2**20),
    )(received, pick, lag_table())


def local(raw_panels, window_start, valid_count, send_rows, pair_slots):
    stations, hours = raw_panels.shape[:2]
    owners, capacity = send_rows.shape[1:]
    pairs = pair_slots.shape[0]
    rows = capacity * PARTS
    hour_devices = lax.axis_size("hour")

    wanted = jnp.broadcast_to(send_rows[0][:, :, None], (owners, capacity, PARTS)).reshape(-1, 1)
    part = jnp.arange(owners * rows, dtype=jnp.int32)[:, None] % PARTS
    source = jnp.arange(PARTS * stations, dtype=jnp.int32)[None, :]
    send_pick = (part * stations + wanted == source).astype(BF16)

    slot = pair_slots.T[:, None, :]
    side_part = jnp.arange(PARTS, dtype=jnp.int32)[None, :, None]
    pair_rows = (slot * PARTS + side_part).reshape(-1, 1)
    arrived = jnp.arange(owners * rows, dtype=jnp.int32)[None, :]
    pair_pick = (pair_rows == arrived).astype(BF16)

    panels = jnp.transpose(raw_panels, (1, 2, 0, 3))
    starts = jnp.transpose(window_start, (1, 2, 0))
    counts = jnp.transpose(valid_count, (1, 2, 0))
    outgoing = whiten(panels, starts, counts, send_pick, owners, rows)
    received = lax.all_to_all(outgoing, "pair", split_axis=0, concat_axis=0, tiled=True)
    partial = correlate(received, pair_pick, pairs, rows, hour_devices)
    shares = lax.all_to_all(partial, "hour", split_axis=0, concat_axis=0, tiled=True)
    average = jnp.sum(shares.astype(F32), axis=0) / (hours * hour_devices)
    size = jnp.abs(average) + 0.1
    stacked = (jnp.sign(average) * (size * size - 0.01)).astype(BF16)
    stacked = lax.all_gather(stacked, "hour", axis=0, tiled=True, axis_index_groups=[list(range(hour_devices))])
    stacked = stacked.reshape(COMPS * COMPS, pairs, LAGS).astype(F32)
    return jnp.transpose(stacked, (1, 0, 2))


def solution(mesh):
    return jax.shard_map(
        local,
        mesh=mesh,
        in_specs=(
            P("pair", "hour", None, None),
            P("pair", "hour", None),
            P("pair", "hour", None),
            P("pair", None, None),
            P("pair", None),
        ),
        out_specs=P("pair", None, None),
        check_vma=False,
    )
```

```python
import functools
import math

import jax
import jax.numpy as jnp
import ml_dtypes
import numpy as np
from jax import lax
from jax.experimental import pallas as pl
from jax.experimental.pallas import tpu as pltpu
from jax.sharding import PartitionSpec as P

NFFT = 1024
NFREQ = 512
LAGS = 256
COMPS = 3
WINDOWS = 2
PARTS = 2 * WINDOWS
SMOOTH_HALF = 11
EPS_WHITE = 1e-06
HALF_HOURS = 4
VMEM_LIMIT = 60 * 2**20
F32 = jnp.float32
BF16 = jnp.bfloat16


def dft_table():
    turns = np.outer(np.arange(NFFT), np.arange(NFREQ)) % NFFT
    angles = turns.astype(np.float32) * np.float32(2.0 * math.pi / NFFT)
    angles = angles.astype(np.float64)
    table = np.concatenate([np.cos(angles), -np.sin(angles)], axis=1)
    return table.astype(np.float32).astype(ml_dtypes.bfloat16)


def band_table():
    index = np.arange(NFREQ)
    band = np.abs(index[:, None] - index[None, :]) <= SMOOTH_HALF
    return band.astype(ml_dtypes.bfloat16)


def lag_table():
    turns = np.outer(np.arange(NFREQ), np.arange(LAGS) - LAGS // 2) % NFFT
    angles = turns.astype(np.float32) * np.float32(2.0 * math.pi / NFFT)
    angles = angles.astype(np.float64)
    weights = np.where(np.arange(NFREQ) == 0, 0.5, 1.0)[:, None]
    table = np.concatenate([weights * np.cos(angles), -weights * np.sin(angles)], axis=0)
    scale = 1.0 / math.sqrt(WINDOWS * NFREQ)
    return (table.astype(np.float32).astype(ml_dtypes.bfloat16) * scale).astype(ml_dtypes.bfloat16)


def column(row, size):
    here = lax.broadcasted_iota(jnp.int32, (size, size), 0)
    there = lax.broadcasted_iota(jnp.int32, (size, size), 1)
    spread = jnp.where(here == there, jnp.broadcast_to(row, (size, size)).astype(F32), 0.0)
    return jnp.sum(spread, axis=1, keepdims=True).astype(jnp.int32)


def cut(panel, start):
    raw = panel.shape[1]
    reach = raw - 2048
    bit = (start & 2048) != 0
    moved = jnp.where(bit, panel[:, 2048:], panel[:, :reach])
    samples = jnp.concatenate([moved, panel[:, reach : NFFT + 2048]], axis=1)
    for size in (1024, 512, 256, 128):
        bit = (start & size) != 0
        keep = NFFT + size
        samples = jnp.where(bit, samples[:, size : size + keep], samples[:, :keep])
    width = samples.shape[1]
    for size in (64, 32, 16, 8, 4, 2, 1):
        bit = (start & size) != 0
        samples = jnp.where(bit, pltpu.roll(samples, width - size, 1), samples)
    return samples[:, :NFFT]


def whiten_kernel(
    raw_hbm, start_ref, count_ref, send_ref, dft_hbm, band_hbm, out_hbm,
    raw_ref, dft_ref, band_ref, seg_ref, spec_ref, white_ref, pick_ref, out_ref, raw_sem, table_sem, out_sem,
):
    hours, _, stations, _ = raw_ref.shape
    capacity, owners = send_ref.shape
    rows = capacity * PARTS
    block = COMPS * WINDOWS * stations
    raw_copies = [pltpu.make_async_copy(raw_hbm.at[h], raw_ref.at[h], raw_sem.at[h]) for h in range(hours)]
    dft_copy = pltpu.make_async_copy(dft_hbm, dft_ref, table_sem.at[0])
    band_copy = pltpu.make_async_copy(band_hbm, band_ref, table_sem.at[1])
    for copy in raw_copies:
        copy.start()
    dft_copy.start()
    band_copy.start()

    out_row = lax.broadcasted_iota(jnp.int32, (owners * rows, owners), 0)
    owner = lax.broadcasted_iota(jnp.int32, (owners * rows, owners), 1)
    spread = (out_row // rows == owner).astype(BF16)
    wanted = lax.dot_general(
        spread, send_ref[...].astype(F32).astype(BF16), (((1,), (1,)), ((), ())), preferred_element_type=F32
    )
    out_row = lax.broadcasted_iota(jnp.int32, (owners * rows, capacity), 0)
    place = lax.broadcasted_iota(jnp.int32, (owners * rows, capacity), 1)
    wanted = jnp.sum(jnp.where(out_row % rows // PARTS == place, wanted, 0.0), axis=1, keepdims=True).astype(jnp.int32)
    out_row = lax.broadcasted_iota(jnp.int32, (owners * rows, PARTS * stations), 0)
    white_row = lax.broadcasted_iota(jnp.int32, (owners * rows, PARTS * stations), 1)
    pick_ref[...] = (out_row % PARTS * stations + wanted == white_row).astype(BF16)

    time = lax.broadcasted_iota(jnp.int32, (stations, NFFT), 1)
    for h in range(hours):
        raw_copies[h].wait()
        for w in range(WINDOWS):
            start = column(start_ref[h, w : w + 1, :], stations)
            count = column(count_ref[h, w : w + 1, :], stations)
            live = time < count
            share = count.astype(F32)
            for c in range(COMPS):
                piece = cut(raw_ref[h, c].astype(F32), start)
                piece = jnp.where(live, piece, 0.0)
                mean = jnp.sum(piece, axis=1, keepdims=True) / share
                row = h * block + (w * COMPS + c) * stations
                seg_ref[row : row + stations, :] = jnp.where(live, piece - mean, 0.0).astype(BF16)
    dft_copy.wait()
    band_copy.wait()
    spec_ref[...] = jnp.dot(seg_ref[...], dft_ref[...], preferred_element_type=F32)
    out_copies = []
    for h in range(hours):
        amps = []
        for w in range(WINDOWS):
            total = jnp.zeros((stations, NFREQ), F32)
            for c in range(COMPS):
                row = h * block + (w * COMPS + c) * stations
                real = spec_ref[row : row + stations, :NFREQ]
                imag = spec_ref[row : row + stations, NFREQ:]
                total = total + jnp.sqrt(real * real + imag * imag)
            amps.append(total)
        amp = jnp.concatenate(amps, axis=0)
        size = WINDOWS * stations
        high = amp.astype(BF16)
        rest = amp - high.astype(F32)
        middle = rest.astype(BF16)
        low = (rest - middle.astype(F32)).astype(BF16)
        sums = jnp.dot(jnp.concatenate([high, middle, low], axis=0), band_ref[...], preferred_element_type=F32)
        smooth = (sums[:size] + sums[size : 2 * size] + sums[2 * size :]) / (3.0 * (2 * SMOOTH_HALF + 1))
        inverse = 1.0 / (smooth + EPS_WHITE)
        for c in range(COMPS):
            cols = slice(c * NFREQ, (c + 1) * NFREQ)
            for w in range(WINDOWS):
                factor = inverse[w * stations : (w + 1) * stations]
                row = h * block + (w * COMPS + c) * stations
                for r in range(2):
                    part = spec_ref[row : row + stations, r * NFREQ : (r + 1) * NFREQ] * factor
                    to = (2 * w + r) * stations
                    white_ref[h, to : to + stations, cols] = part.astype(BF16)
            picked = jnp.dot(pick_ref[...], white_ref[h, :, cols], preferred_element_type=F32).astype(BF16)
            out_ref[h, :, :, cols] = picked.reshape(owners, rows, NFREQ)
        copy = pltpu.make_async_copy(out_ref.at[h], out_hbm.at[:, pl.ds(h * rows, rows), :], out_sem.at[h])
        copy.start()
        out_copies.append(copy)
    for copy in out_copies:
        copy.wait()


def correlate_kernel(recv_ref, pick_ref, lag_ref, out_ref, side_ref, cross_ref, total_ref):
    hour = pl.program_id(0)
    pairs = total_ref.shape[0] // (COMPS * COMPS)
    slots = recv_ref.shape[0] * recv_ref.shape[1]
    width = recv_ref.shape[2]
    for c in range(COMPS):
        cols = slice(c * NFREQ, (c + 1) * NFREQ)
        arrived = recv_ref[:, :, cols].reshape(slots, NFREQ)
        side_ref[:, cols] = jnp.dot(pick_ref[...], arrived, preferred_element_type=F32)

    for k in range(0, pairs, 16):
        for f in range(0, NFREQ, 128):
            def load(side, part, comp):
                row = (side * PARTS + part) * pairs + k
                col = comp * NFREQ + f
                return side_ref[row : row + 16, col : col + 128]
            left = [[load(0, part, comp) for comp in range(COMPS)] for part in range(PARTS)]
            right = [[load(1, part, comp) for comp in range(COMPS)] for part in range(PARTS)]
            for i in range(COMPS):
                for j in range(COMPS):
                    real = left[0][i] * right[0][j] + left[2][i] * right[2][j]
                    real = real + (left[1][i] * right[1][j] + left[3][i] * right[3][j])
                    imag = left[1][i] * right[0][j] + left[3][i] * right[2][j]
                    imag = imag - (left[0][i] * right[1][j] + left[2][i] * right[3][j])
                    row = (COMPS * i + j) * pairs + k
                    cross_ref[row : row + 16, f : f + 128] = real.astype(BF16)
                    cross_ref[row : row + 16, NFREQ + f : NFREQ + f + 128] = imag.astype(BF16)
    lagged = jnp.dot(cross_ref[...], lag_ref[...], preferred_element_type=F32)
    root = jnp.sqrt(jnp.abs(lagged) + 0.01) - 0.1
    root = jnp.where(lagged > 0.0, root, jnp.where(lagged < 0.0, -root, 0.0))

    @pl.when(hour == 0)
    def _():
        total_ref[...] = root

    @pl.when(hour > 0)
    def _():
        total_ref[...] += root

    @pl.when(hour == pl.num_programs(0) - 1)
    def _():
        out_ref[...] = total_ref[...].astype(BF16).reshape(out_ref.shape)


def whiten(panels, starts, counts, send):
    hours, _, stations, raw = panels.shape
    capacity, owners = send.shape
    rows = capacity * PARTS
    width = COMPS * NFREQ
    block = WINDOWS * COMPS * stations
    hbm = pl.BlockSpec(memory_space=pltpu.HBM)
    vmem = pl.BlockSpec(memory_space=pltpu.VMEM)
    return pl.pallas_call(
        whiten_kernel,
        in_specs=[hbm, vmem, vmem, vmem, hbm, hbm],
        out_specs=hbm,
        out_shape=jax.ShapeDtypeStruct((owners, hours * rows, width), BF16),
        scratch_shapes=[
            pltpu.VMEM(panels.shape, BF16),
            pltpu.VMEM((NFFT, 2 * NFREQ), BF16),
            pltpu.VMEM((NFREQ, NFREQ), BF16),
            pltpu.VMEM((hours * block, NFFT), BF16),
            pltpu.VMEM((hours * block, 2 * NFREQ), F32),
            pltpu.VMEM((hours, PARTS * stations, width), BF16),
            pltpu.VMEM((owners * rows, PARTS * stations), BF16),
            pltpu.VMEM((hours, owners, rows, width), BF16),
            pltpu.SemaphoreType.DMA((hours,)),
            pltpu.SemaphoreType.DMA((2,)),
            pltpu.SemaphoreType.DMA((hours,)),
        ],
        compiler_params=pltpu.CompilerParams(vmem_limit_bytes=VMEM_LIMIT),
    )(panels, starts, counts, send, dft_table(), band_table())


def gather_kernel(*refs):
    part_refs, out_ref = refs[:-1], refs[-1]
    me = lax.axis_index("hour")
    for k, part_ref in enumerate(part_refs):
        for far in range(2):
            out_ref[me ^ (k + HALF_HOURS * far)] = part_ref[far].astype(F32)


def gather(mine):
    def swap(array, distance):
        return lax.ppermute(array, "hour", [(i, i ^ distance) for i in range(2 * HALF_HOURS)])

    both = jnp.stack([mine, swap(mine, HALF_HOURS)])
    parts = [both] + [swap(both, k) for k in range(1, HALF_HOURS)]
    return pl.pallas_call(
        gather_kernel,
        out_shape=jax.ShapeDtypeStruct((2 * HALF_HOURS,) + mine.shape, F32),
        name="spread_result",
    )(*parts)


def correlate(received, pick, pairs, rows, pieces):
    owners, all_rows, width = received.shape
    hours = all_rows // rows
    channels = COMPS * COMPS
    whole = lambda shape: pl.BlockSpec(shape, lambda h: (0,) * len(shape))
    piece = (pieces, channels * pairs // pieces, LAGS)
    return pl.pallas_call(
        correlate_kernel,
        grid=(hours,),
        in_specs=[
            pl.BlockSpec((owners, rows, width), lambda h: (0, h, 0)),
            whole(pick.shape),
            whole((2 * NFREQ, LAGS)),
        ],
        out_specs=whole(piece),
        out_shape=jax.ShapeDtypeStruct(piece, BF16),
        scratch_shapes=[
            pltpu.VMEM((2 * PARTS * pairs, width), F32),
            pltpu.VMEM((channels * pairs, 2 * NFREQ), BF16),
            pltpu.VMEM((channels * pairs, LAGS), F32),
        ],
        compiler_params=pltpu.CompilerParams(vmem_limit_bytes=VMEM_LIMIT),
    )(received, pick, lag_table())


def local(raw_panels, window_start, valid_count, send_rows, pair_slots):
    stations, hours = raw_panels.shape[:2]
    owners, capacity = send_rows.shape[1:]
    pairs = pair_slots.shape[0]
    rows = capacity * PARTS
    hour_devices = lax.axis_size("hour")

    slot = pair_slots.T[:, None, :]
    side_part = jnp.arange(PARTS, dtype=jnp.int32)[None, :, None]
    pair_rows = (slot * PARTS + side_part).reshape(-1, 1)
    arrived = jnp.arange(owners * rows, dtype=jnp.int32)[None, :]
    pair_pick = (pair_rows == arrived).astype(BF16)

    panels = jnp.transpose(raw_panels, (1, 2, 0, 3))
    starts = jnp.transpose(window_start, (1, 2, 0))
    counts = jnp.transpose(valid_count, (1, 2, 0))
    outgoing = whiten(panels, starts, counts, jnp.transpose(send_rows[0]))
    received = lax.all_to_all(outgoing, "pair", split_axis=0, concat_axis=0, tiled=True)
    partial = correlate(received, pair_pick, pairs, rows, hour_devices)
    shares = lax.all_to_all(partial, "hour", split_axis=0, concat_axis=0, tiled=True)
    average = jnp.sum(shares.astype(F32), axis=0) / (hours * hour_devices)
    size = jnp.abs(average) + 0.1
    stacked = (jnp.sign(average) * (size * size - 0.01)).astype(BF16)
    stacked = gather(stacked).reshape(COMPS * COMPS, pairs, LAGS)
    return jnp.transpose(stacked, (1, 0, 2))


def solution(mesh):
    return jax.shard_map(
        local,
        mesh=mesh,
        in_specs=(
            P("pair", "hour", None, None),
            P("pair", "hour", None),
            P("pair", "hour", None),
            P("pair", None, None),
            P("pair", None),
        ),
        out_specs=P("pair", None, None),
        check_vma=False,
    )
```

```python
import functools
import math

import jax
import jax.numpy as jnp
import ml_dtypes
import numpy as np
from jax import lax
from jax.experimental import pallas as pl
from jax.experimental.pallas import tpu as pltpu
from jax.sharding import PartitionSpec as P

NFFT = 1024
NFREQ = 512
LAGS = 256
COMPS = 3
WINDOWS = 2
PARTS = 2 * WINDOWS
SMOOTH_HALF = 11
EPS_WHITE = 1e-06
HALF_HOURS = 4
WHITEN_VMEM = 58 * 2**20
CORRELATE_VMEM = 24 * 2**20
SPREAD_VMEM = 8 * 2**20
F32 = jnp.float32
BF16 = jnp.bfloat16


def dft_table():
    turns = np.outer(np.arange(NFFT), np.arange(NFREQ)) % NFFT
    angles = turns.astype(np.float32) * np.float32(2.0 * math.pi / NFFT)
    angles = angles.astype(np.float64)
    table = np.concatenate([np.cos(angles), -np.sin(angles)], axis=1)
    return table.astype(np.float32).astype(ml_dtypes.bfloat16)


def band_table():
    index = np.arange(NFREQ)
    band = np.abs(index[:, None] - index[None, :]) <= SMOOTH_HALF
    return band.astype(ml_dtypes.bfloat16)


def lag_table():
    turns = np.outer(np.arange(NFREQ), np.arange(LAGS) - LAGS // 2) % NFFT
    angles = turns.astype(np.float32) * np.float32(2.0 * math.pi / NFFT)
    angles = angles.astype(np.float64)
    weights = np.where(np.arange(NFREQ) == 0, 0.5, 1.0)[:, None]
    table = np.concatenate([weights * np.cos(angles), -weights * np.sin(angles)], axis=0)
    scale = 1.0 / math.sqrt(WINDOWS * NFREQ)
    return (table.astype(np.float32).astype(ml_dtypes.bfloat16) * scale).astype(ml_dtypes.bfloat16)


def column(row, size):
    here = lax.broadcasted_iota(jnp.int32, (size, size), 0)
    there = lax.broadcasted_iota(jnp.int32, (size, size), 1)
    spread = jnp.where(here == there, jnp.broadcast_to(row, (size, size)).astype(F32), 0.0)
    return jnp.sum(spread, axis=1, keepdims=True).astype(jnp.int32)


def cut(panel, start):
    raw = panel.shape[1]
    reach = raw - 2048
    bit = (start & 2048) != 0
    moved = jnp.where(bit, panel[:, 2048:], panel[:, :reach])
    samples = jnp.concatenate([moved, panel[:, reach : NFFT + 2048]], axis=1)
    for size in (1024, 512, 256, 128):
        bit = (start & size) != 0
        keep = NFFT + size
        samples = jnp.where(bit, samples[:, size : size + keep], samples[:, :keep])
    width = samples.shape[1]
    for size in (64, 32, 16, 8, 4, 2, 1):
        bit = (start & size) != 0
        samples = jnp.where(bit, pltpu.roll(samples, width - size, 1), samples)
    return samples[:, :NFFT]


def whiten_kernel(
    raw_hbm, start_hbm, count_hbm, send_hbm, dft_hbm, band_hbm, out_hbm,
    raw_ref, start_ref, count_ref, send_ref, dft_ref, band_ref, seg_ref, spec_ref, white_ref, pick_ref, out_ref,
    small_sem, raw_sem, table_sem, out_sem,
):
    hours, _, stations, _ = raw_ref.shape
    capacity, owners = send_ref.shape
    rows = capacity * PARTS
    block = COMPS * WINDOWS * stations
    small_copies = [
        pltpu.make_async_copy(start_hbm, start_ref, small_sem.at[0]),
        pltpu.make_async_copy(count_hbm, count_ref, small_sem.at[1]),
        pltpu.make_async_copy(send_hbm, send_ref, small_sem.at[2]),
    ]
    raw_copies = [pltpu.make_async_copy(raw_hbm.at[h], raw_ref.at[h], raw_sem.at[h]) for h in range(hours)]
    dft_copy = pltpu.make_async_copy(dft_hbm, dft_ref, table_sem.at[0])
    band_copy = pltpu.make_async_copy(band_hbm, band_ref, table_sem.at[1])
    for copy in small_copies + raw_copies:
        copy.start()
    dft_copy.start()
    band_copy.start()
    for copy in small_copies:
        copy.wait()

    out_row = lax.broadcasted_iota(jnp.int32, (owners * rows, owners), 0)
    owner = lax.broadcasted_iota(jnp.int32, (owners * rows, owners), 1)
    spread = (out_row // rows == owner).astype(BF16)
    wanted = lax.dot_general(
        spread, send_ref[...].astype(F32).astype(BF16), (((1,), (1,)), ((), ())), preferred_element_type=F32
    )
    out_row = lax.broadcasted_iota(jnp.int32, (owners * rows, capacity), 0)
    place = lax.broadcasted_iota(jnp.int32, (owners * rows, capacity), 1)
    wanted = jnp.sum(jnp.where(out_row % rows // PARTS == place, wanted, 0.0), axis=1, keepdims=True).astype(jnp.int32)
    out_row = lax.broadcasted_iota(jnp.int32, (owners * rows, PARTS * stations), 0)
    white_row = lax.broadcasted_iota(jnp.int32, (owners * rows, PARTS * stations), 1)
    pick_ref[...] = (out_row % PARTS * stations + wanted == white_row).astype(BF16)

    time = lax.broadcasted_iota(jnp.int32, (stations, NFFT), 1)
    for h in range(hours):
        raw_copies[h].wait()
        for w in range(WINDOWS):
            start = column(start_ref[h, w : w + 1, :], stations)
            count = column(count_ref[h, w : w + 1, :], stations)
            live = time < count
            share = count.astype(F32)
            for c in range(COMPS):
                piece = cut(raw_ref[h, c].astype(F32), start)
                piece = jnp.where(live, piece, 0.0)
                mean = jnp.sum(piece, axis=1, keepdims=True) / share
                row = h * block + (w * COMPS + c) * stations
                seg_ref[row : row + stations, :] = jnp.where(live, piece - mean, 0.0).astype(BF16)
    dft_copy.wait()
    band_copy.wait()
    out_copies = []
    spec_ref[...] = jnp.dot(seg_ref[...], dft_ref[...], preferred_element_type=F32)
    for h in range(hours):
        amps = []
        for w in range(WINDOWS):
            total = jnp.zeros((stations, NFREQ), F32)
            for c in range(COMPS):
                row = h * block + (w * COMPS + c) * stations
                real = spec_ref[row : row + stations, :NFREQ]
                imag = spec_ref[row : row + stations, NFREQ:]
                total = total + jnp.sqrt(real * real + imag * imag)
            amps.append(total)
        amp = jnp.concatenate(amps, axis=0)
        size = WINDOWS * stations
        high = amp.astype(BF16)
        rest = amp - high.astype(F32)
        middle = rest.astype(BF16)
        low = (rest - middle.astype(F32)).astype(BF16)
        sums = jnp.dot(jnp.concatenate([high, middle, low], axis=0), band_ref[...], preferred_element_type=F32)
        smooth = (sums[:size] + sums[size : 2 * size] + sums[2 * size :]) / (3.0 * (2 * SMOOTH_HALF + 1))
        inverse = 1.0 / (smooth + EPS_WHITE)
        for c in range(COMPS):
            cols = slice(c * NFREQ, (c + 1) * NFREQ)
            for w in range(WINDOWS):
                factor = inverse[w * stations : (w + 1) * stations]
                row = h * block + (w * COMPS + c) * stations
                for r in range(2):
                    part = spec_ref[row : row + stations, r * NFREQ : (r + 1) * NFREQ] * factor
                    to = (2 * w + r) * stations
                    white_ref[h, to : to + stations, cols] = part.astype(BF16)
            picked = jnp.dot(pick_ref[...], white_ref[h, :, cols], preferred_element_type=F32).astype(BF16)
            out_ref[h, :, :, cols] = picked.reshape(owners, rows, NFREQ)
        copy = pltpu.make_async_copy(out_ref.at[h], out_hbm.at[:, pl.ds(h * rows, rows), :], out_sem.at[h])
        copy.start()
        out_copies.append(copy)
    for copy in out_copies:
        copy.wait()


def correlate_kernel(recv_ref, slots_ref, lag_hbm, out_ref, pick_ref, lag_ref, side_ref, cross_ref, total_ref, sem):
    pairs = slots_ref.shape[1]
    owners, all_rows, _ = recv_ref.shape
    rows = all_rows // cross_ref.shape[0]
    half = NFREQ // 2
    lag_copy = pltpu.make_async_copy(lag_hbm, lag_ref, sem)
    lag_copy.start()

    arrived_row = lax.broadcasted_iota(jnp.int32, (pairs, owners * rows), 1)
    for side in range(2):
        first = column(slots_ref[side : side + 1, :], pairs) * PARTS
        for part in range(PARTS):
            row = (side * PARTS + part) * pairs
            pick_ref[row : row + pairs, :] = (first + part == arrived_row).astype(BF16)

    def select(h, n):
        for c in range(COMPS):
            col = c * NFREQ + n * half
            arrived = recv_ref[:, h * rows : (h + 1) * rows, col : col + half].reshape(owners * rows, half)
            side_ref[n, :, c * half : (c + 1) * half] = jnp.dot(pick_ref[...], arrived, preferred_element_type=F32)

    def cross(h, n):
        for k in range(0, pairs, 16):
            for f in range(0, half, 128):
                def load(side, part, comp):
                    row = (side * PARTS + part) * pairs + k
                    col = comp * half + f
                    return side_ref[n, row : row + 16, col : col + 128]
                left = [[load(0, part, comp) for comp in range(COMPS)] for part in range(PARTS)]
                right = [[load(1, part, comp) for comp in range(COMPS)] for part in range(PARTS)]
                for i in range(COMPS):
                    for j in range(COMPS):
                        real = left[0][i] * right[0][j] + left[2][i] * right[2][j]
                        real = real + (left[1][i] * right[1][j] + left[3][i] * right[3][j])
                        imag = left[1][i] * right[0][j] + left[3][i] * right[2][j]
                        imag = imag - (left[0][i] * right[1][j] + left[2][i] * right[3][j])
                        row = (COMPS * i + j) * pairs + k
                        col = n * half + f
                        cross_ref[h, row : row + 16, col : col + 128] = real.astype(BF16)
                        cross_ref[h, row : row + 16, NFREQ + col : NFREQ + col + 128] = imag.astype(BF16)

    def root(h):
        lagged = jnp.dot(cross_ref[h], lag_ref[...], preferred_element_type=F32)
        rooted = jnp.sqrt(jnp.abs(lagged) + 0.01) - 0.1
        rooted = jnp.where(lagged > 0.0, rooted, jnp.where(lagged < 0.0, -rooted, 0.0))
        if h == 0:
            total_ref[...] = rooted
        elif h < cross_ref.shape[0] - 1:
            total_ref[...] += rooted
        else:
            out_ref[...] = (total_ref[...] + rooted).astype(BF16).reshape(out_ref.shape)

    lag_copy.wait()
    for h in range(cross_ref.shape[0]):
        for n in range(2):
            select(h, n)
            cross(h, n)
        root(h)


def whiten(panels, starts, counts, send):
    hours, _, stations, raw = panels.shape
    capacity, owners = send.shape
    rows = capacity * PARTS
    width = COMPS * NFREQ
    block = WINDOWS * COMPS * stations
    hbm = pl.BlockSpec(memory_space=pltpu.HBM)
    return pl.pallas_call(
        whiten_kernel,
        in_specs=[hbm] * 6,
        out_specs=hbm,
        out_shape=jax.ShapeDtypeStruct((owners, hours * rows, width), BF16),
        scratch_shapes=[
            pltpu.VMEM(panels.shape, BF16),
            pltpu.VMEM(starts.shape, jnp.int32),
            pltpu.VMEM(counts.shape, jnp.int32),
            pltpu.VMEM(send.shape, jnp.int32),
            pltpu.VMEM((NFFT, 2 * NFREQ), BF16),
            pltpu.VMEM((NFREQ, NFREQ), BF16),
            pltpu.VMEM((hours * block, NFFT), BF16),
            pltpu.VMEM((hours * block, 2 * NFREQ), F32),
            pltpu.VMEM((hours, PARTS * stations, width), BF16),
            pltpu.VMEM((owners * rows, PARTS * stations), BF16),
            pltpu.VMEM((hours, owners, rows, width), BF16),
            pltpu.SemaphoreType.DMA((3,)),
            pltpu.SemaphoreType.DMA((hours,)),
            pltpu.SemaphoreType.DMA((2,)),
            pltpu.SemaphoreType.DMA((hours,)),
        ],
        compiler_params=pltpu.CompilerParams(vmem_limit_bytes=WHITEN_VMEM),
    )(panels, starts, counts, send, dft_table(), band_table())


def gather_kernel(*refs):
    part_refs, out_ref = refs[:-1], refs[-1]
    me = lax.axis_index("hour")
    for k, part_ref in enumerate(part_refs):
        for far in range(2):
            out_ref[me ^ (k + HALF_HOURS * far)] = part_ref[far].astype(F32)


def gather(mine):
    def swap(array, distance):
        return lax.ppermute(array, "hour", [(i, i ^ distance) for i in range(2 * HALF_HOURS)])

    both = jnp.stack([mine, swap(mine, HALF_HOURS)])
    parts = [both] + [swap(both, k) for k in range(1, HALF_HOURS)]
    return pl.pallas_call(
        gather_kernel,
        out_shape=jax.ShapeDtypeStruct((2 * HALF_HOURS,) + mine.shape, F32),
        compiler_params=pltpu.CompilerParams(vmem_limit_bytes=SPREAD_VMEM),
        name="spread_result",
    )(*parts)


def correlate(received, slots, hours, pieces):
    owners, all_rows, width = received.shape
    pairs = slots.shape[1]
    rows = all_rows // hours
    channels = COMPS * COMPS
    vmem = pl.BlockSpec(memory_space=pltpu.VMEM)
    return pl.pallas_call(
        correlate_kernel,
        in_specs=[vmem, vmem, pl.BlockSpec(memory_space=pltpu.HBM)],
        out_specs=vmem,
        out_shape=jax.ShapeDtypeStruct((pieces, channels * pairs // pieces, LAGS), BF16),
        scratch_shapes=[
            pltpu.VMEM((2 * PARTS * pairs, owners * rows), BF16),
            pltpu.VMEM((2 * NFREQ, LAGS), BF16),
            pltpu.VMEM((2, 2 * PARTS * pairs, width // 2), F32),
            pltpu.VMEM((hours, channels * pairs, 2 * NFREQ), BF16),
            pltpu.VMEM((channels * pairs, LAGS), F32),
            pltpu.SemaphoreType.DMA(()),
        ],
        compiler_params=pltpu.CompilerParams(vmem_limit_bytes=CORRELATE_VMEM),
    )(received, slots, lag_table())


def local(raw_panels, window_start, valid_count, send_rows, pair_slots):
    hours = raw_panels.shape[1]
    pairs = pair_slots.shape[0]
    hour_devices = lax.axis_size("hour")
    panels = jnp.transpose(raw_panels, (1, 2, 0, 3))
    starts = jnp.transpose(window_start, (1, 2, 0))
    counts = jnp.transpose(valid_count, (1, 2, 0))
    outgoing = whiten(panels, starts, counts, jnp.transpose(send_rows[0]))
    received = lax.all_to_all(outgoing, "pair", split_axis=0, concat_axis=0, tiled=True)
    partial = correlate(received, jnp.transpose(pair_slots), hours, hour_devices)
    shares = lax.all_to_all(partial, "hour", split_axis=0, concat_axis=0, tiled=True)
    average = jnp.sum(shares.astype(F32), axis=0) / (hours * hour_devices)
    size = jnp.abs(average) + 0.1
    stacked = (jnp.sign(average) * (size * size - 0.01)).astype(BF16)
    stacked = gather(stacked).reshape(COMPS * COMPS, pairs, LAGS)
    return jnp.transpose(stacked, (1, 0, 2))


def solution(mesh):
    return jax.shard_map(
        local,
        mesh=mesh,
        in_specs=(
            P("pair", "hour", None, None),
            P("pair", "hour", None),
            P("pair", "hour", None),
            P("pair", None, None),
            P("pair", None),
        ),
        out_specs=P("pair", None, None),
        check_vma=False,
    )
```

```python
import functools
import math

import jax
import jax.numpy as jnp
import ml_dtypes
import numpy as np
from jax import lax
from jax.experimental import pallas as pl
from jax.experimental.pallas import tpu as pltpu
from jax.sharding import PartitionSpec as P

NFFT = 1024
NFREQ = 512
LAGS = 256
COMPS = 3
WINDOWS = 2
PARTS = 2 * WINDOWS
SMOOTH_HALF = 11
EPS_WHITE = 1e-06
HALF_HOURS = 4
WHITEN_VMEM = 58 * 2**20
CORRELATE_VMEM = 24 * 2**20
SPREAD_VMEM = 8 * 2**20
F32 = jnp.float32
BF16 = jnp.bfloat16


def dft_table():
    turns = np.outer(np.arange(NFFT), np.arange(NFREQ)) % NFFT
    angles = turns.astype(np.float32) * np.float32(2.0 * math.pi / NFFT)
    angles = angles.astype(np.float64)
    table = np.concatenate([np.cos(angles), -np.sin(angles)], axis=1)
    return table.astype(np.float32).astype(ml_dtypes.bfloat16)


def band_table():
    index = np.arange(NFREQ)
    band = np.abs(index[:, None] - index[None, :]) <= SMOOTH_HALF
    return band.astype(ml_dtypes.bfloat16)


def lag_table():
    turns = np.outer(np.arange(NFREQ), np.arange(LAGS) - LAGS // 2) % NFFT
    angles = turns.astype(np.float32) * np.float32(2.0 * math.pi / NFFT)
    angles = angles.astype(np.float64)
    weights = np.where(np.arange(NFREQ) == 0, 0.5, 1.0)[:, None]
    table = np.concatenate([weights * np.cos(angles), -weights * np.sin(angles)], axis=0)
    scale = 1.0 / math.sqrt(WINDOWS * NFREQ)
    return (table.astype(np.float32).astype(ml_dtypes.bfloat16) * scale).astype(ml_dtypes.bfloat16)


def column(row, size):
    here = lax.broadcasted_iota(jnp.int32, (size, size), 0)
    there = lax.broadcasted_iota(jnp.int32, (size, size), 1)
    spread = jnp.where(here == there, jnp.broadcast_to(row, (size, size)).astype(F32), 0.0)
    return jnp.sum(spread, axis=1, keepdims=True).astype(jnp.int32)


def cut(panel, start):
    raw = panel.shape[1]
    reach = raw - 2048
    bit = (start & 2048) != 0
    moved = jnp.where(bit, panel[:, 2048:], panel[:, :reach])
    samples = jnp.concatenate([moved, panel[:, reach : NFFT + 2048]], axis=1)
    for size in (1024, 512, 256, 128):
        bit = (start & size) != 0
        keep = NFFT + size
        samples = jnp.where(bit, samples[:, size : size + keep], samples[:, :keep])
    width = samples.shape[1]
    for size in (64, 32, 16, 8, 4, 2, 1):
        bit = (start & size) != 0
        samples = jnp.where(bit, pltpu.roll(samples, width - size, 1), samples)
    return samples[:, :NFFT]


def whiten_kernel(
    raw_hbm, start_hbm, count_hbm, send_hbm, dft_hbm, band_hbm, out_hbm,
    raw_ref, start_ref, count_ref, send_ref, dft_ref, band_ref, seg_ref, spec_ref, white_ref, pick_ref, out_ref,
    small_sem, raw_sem, table_sem, out_sem,
):
    hours, _, stations, _ = raw_ref.shape
    capacity, owners = send_ref.shape
    rows = capacity * PARTS
    block = COMPS * WINDOWS * stations
    small_copies = [
        pltpu.make_async_copy(start_hbm, start_ref, small_sem.at[0]),
        pltpu.make_async_copy(count_hbm, count_ref, small_sem.at[1]),
        pltpu.make_async_copy(send_hbm, send_ref, small_sem.at[2]),
    ]
    raw_copies = [pltpu.make_async_copy(raw_hbm.at[h], raw_ref.at[h], raw_sem.at[h]) for h in range(hours)]
    dft_copy = pltpu.make_async_copy(dft_hbm, dft_ref, table_sem.at[0])
    band_copy = pltpu.make_async_copy(band_hbm, band_ref, table_sem.at[1])
    for copy in small_copies + raw_copies:
        copy.start()
    dft_copy.start()
    band_copy.start()
    for copy in small_copies:
        copy.wait()

    out_row = lax.broadcasted_iota(jnp.int32, (owners * rows, owners), 0)
    owner = lax.broadcasted_iota(jnp.int32, (owners * rows, owners), 1)
    spread = (out_row // rows == owner).astype(BF16)
    wanted = lax.dot_general(
        spread, send_ref[...].astype(F32).astype(BF16), (((1,), (1,)), ((), ())), preferred_element_type=F32
    )
    out_row = lax.broadcasted_iota(jnp.int32, (owners * rows, capacity), 0)
    place = lax.broadcasted_iota(jnp.int32, (owners * rows, capacity), 1)
    wanted = jnp.sum(jnp.where(out_row % rows // PARTS == place, wanted, 0.0), axis=1, keepdims=True).astype(jnp.int32)
    out_row = lax.broadcasted_iota(jnp.int32, (owners * rows, PARTS * stations), 0)
    white_row = lax.broadcasted_iota(jnp.int32, (owners * rows, PARTS * stations), 1)
    pick_ref[...] = (out_row % PARTS * stations + wanted == white_row).astype(BF16)

    time = lax.broadcasted_iota(jnp.int32, (stations, NFFT), 1)
    for h in range(hours):
        raw_copies[h].wait()
        for w in range(WINDOWS):
            start = column(start_ref[h, w : w + 1, :], stations)
            count = column(count_ref[h, w : w + 1, :], stations)
            live = time < count
            share = count.astype(F32)
            for c in range(COMPS):
                piece = cut(raw_ref[h, c].astype(F32), start)
                piece = jnp.where(live, piece, 0.0)
                mean = jnp.sum(piece, axis=1, keepdims=True) / share
                row = h * block + (w * COMPS + c) * stations
                seg_ref[row : row + stations, :] = jnp.where(live, piece - mean, 0.0).astype(BF16)
    dft_copy.wait()
    band_copy.wait()
    out_copies = []
    spec_ref[...] = jnp.dot(seg_ref[...], dft_ref[...], preferred_element_type=F32)
    for h in range(hours):
        amps = []
        for w in range(WINDOWS):
            total = jnp.zeros((stations, NFREQ), F32)
            for c in range(COMPS):
                row = h * block + (w * COMPS + c) * stations
                real = spec_ref[row : row + stations, :NFREQ]
                imag = spec_ref[row : row + stations, NFREQ:]
                total = total + jnp.sqrt(real * real + imag * imag)
            amps.append(total)
        amp = jnp.concatenate(amps, axis=0)
        size = WINDOWS * stations
        high = amp.astype(BF16)
        rest = amp - high.astype(F32)
        middle = rest.astype(BF16)
        low = (rest - middle.astype(F32)).astype(BF16)
        sums = jnp.dot(jnp.concatenate([high, middle, low], axis=0), band_ref[...], preferred_element_type=F32)
        smooth = (sums[:size] + sums[size : 2 * size] + sums[2 * size :]) / (3.0 * (2 * SMOOTH_HALF + 1))
        inverse = 1.0 / (smooth + EPS_WHITE)
        for c in range(COMPS):
            cols = slice(c * NFREQ, (c + 1) * NFREQ)
            for w in range(WINDOWS):
                factor = inverse[w * stations : (w + 1) * stations]
                row = h * block + (w * COMPS + c) * stations
                for r in range(2):
                    part = spec_ref[row : row + stations, r * NFREQ : (r + 1) * NFREQ] * factor
                    to = (2 * w + r) * stations
                    white_ref[h, to : to + stations, cols] = part.astype(BF16)
            picked = jnp.dot(pick_ref[...], white_ref[h, :, cols], preferred_element_type=F32).astype(BF16)
            out_ref[h, :, :, cols] = picked.reshape(owners, rows, NFREQ)
        copy = pltpu.make_async_copy(out_ref.at[h], out_hbm.at[:, pl.ds(h * rows, rows), :], out_sem.at[h])
        copy.start()
        out_copies.append(copy)
    for copy in out_copies:
        copy.wait()


def share_of(device):
    return jnp.minimum(device, 2 * HALF_HOURS - 1 - device)


def correlate_kernel(recv_ref, slots_ref, lag_hbm, *refs):
    out_refs, (pick_ref, lag_ref, side_ref, cross_ref, total_ref, sem) = refs[:HALF_HOURS], refs[HALF_HOURS:]
    pairs = slots_ref.shape[1]
    owners, all_rows, _ = recv_ref.shape
    rows = all_rows // cross_ref.shape[0]
    half = NFREQ // 2
    lag_copy = pltpu.make_async_copy(lag_hbm, lag_ref, sem)
    lag_copy.start()

    arrived_row = lax.broadcasted_iota(jnp.int32, (pairs, owners * rows), 1)
    for side in range(2):
        first = column(slots_ref[side : side + 1, :], pairs) * PARTS
        for part in range(PARTS):
            row = (side * PARTS + part) * pairs
            pick_ref[row : row + pairs, :] = (first + part == arrived_row).astype(BF16)

    def select(h, n):
        for c in range(COMPS):
            col = c * NFREQ + n * half
            arrived = recv_ref[:, h * rows : (h + 1) * rows, col : col + half].reshape(owners * rows, half)
            side_ref[n, :, c * half : (c + 1) * half] = jnp.dot(pick_ref[...], arrived, preferred_element_type=F32)

    def cross(h, n):
        for k in range(0, pairs, 16):
            for f in range(0, half, 128):
                def load(side, part, comp):
                    row = (side * PARTS + part) * pairs + k
                    col = comp * half + f
                    return side_ref[n, row : row + 16, col : col + 128]
                left = [[load(0, part, comp) for comp in range(COMPS)] for part in range(PARTS)]
                right = [[load(1, part, comp) for comp in range(COMPS)] for part in range(PARTS)]
                for i in range(COMPS):
                    for j in range(COMPS):
                        real = left[0][i] * right[0][j] + left[2][i] * right[2][j]
                        real = real + (left[1][i] * right[1][j] + left[3][i] * right[3][j])
                        imag = left[1][i] * right[0][j] + left[3][i] * right[2][j]
                        imag = imag - (left[0][i] * right[1][j] + left[2][i] * right[3][j])
                        row = (COMPS * i + j) * pairs + k
                        col = n * half + f
                        cross_ref[h, row : row + 16, col : col + 128] = real.astype(BF16)
                        cross_ref[h, row : row + 16, NFREQ + col : NFREQ + col + 128] = imag.astype(BF16)

    def root(h):
        lagged = jnp.dot(cross_ref[h], lag_ref[...], preferred_element_type=F32)
        rooted = jnp.sqrt(jnp.abs(lagged) + 0.01) - 0.1
        rooted = jnp.where(lagged > 0.0, rooted, jnp.where(lagged < 0.0, -rooted, 0.0))
        rooted = rooted.reshape(total_ref.shape)
        if h == 0:
            total_ref[...] = rooted
        else:
            total_ref[...] += rooted

    lag_copy.wait()
    for h in range(cross_ref.shape[0]):
        for n in range(2):
            select(h, n)
            cross(h, n)
        root(h)
    me = lax.axis_index("hour")
    for k, out_ref in enumerate(out_refs):
        out_ref[...] = total_ref[share_of(me ^ k)].astype(BF16)


def whiten(panels, starts, counts, send):
    hours, _, stations, raw = panels.shape
    capacity, owners = send.shape
    rows = capacity * PARTS
    width = COMPS * NFREQ
    block = WINDOWS * COMPS * stations
    hbm = pl.BlockSpec(memory_space=pltpu.HBM)
    return pl.pallas_call(
        whiten_kernel,
        in_specs=[hbm] * 6,
        out_specs=hbm,
        out_shape=jax.ShapeDtypeStruct((owners, hours * rows, width), BF16),
        scratch_shapes=[
            pltpu.VMEM(panels.shape, BF16),
            pltpu.VMEM(starts.shape, jnp.int32),
            pltpu.VMEM(counts.shape, jnp.int32),
            pltpu.VMEM(send.shape, jnp.int32),
            pltpu.VMEM((NFFT, 2 * NFREQ), BF16),
            pltpu.VMEM((NFREQ, NFREQ), BF16),
            pltpu.VMEM((hours * block, NFFT), BF16),
            pltpu.VMEM((hours * block, 2 * NFREQ), F32),
            pltpu.VMEM((hours, PARTS * stations, width), BF16),
            pltpu.VMEM((owners * rows, PARTS * stations), BF16),
            pltpu.VMEM((hours, owners, rows, width), BF16),
            pltpu.SemaphoreType.DMA((3,)),
            pltpu.SemaphoreType.DMA((hours,)),
            pltpu.SemaphoreType.DMA((2,)),
            pltpu.SemaphoreType.DMA((hours,)),
        ],
        compiler_params=pltpu.CompilerParams(vmem_limit_bytes=WHITEN_VMEM),
    )(panels, starts, counts, send, dft_table(), band_table())


def correlate(received, slots, hours):
    owners, all_rows, width = received.shape
    pairs = slots.shape[1]
    rows = all_rows // hours
    channels = COMPS * COMPS
    vmem = pl.BlockSpec(memory_space=pltpu.VMEM)
    share = (channels * pairs // HALF_HOURS, LAGS)
    return pl.pallas_call(
        correlate_kernel,
        in_specs=[vmem, vmem, pl.BlockSpec(memory_space=pltpu.HBM)],
        out_specs=[vmem] * HALF_HOURS,
        out_shape=[jax.ShapeDtypeStruct(share, BF16)] * HALF_HOURS,
        scratch_shapes=[
            pltpu.VMEM((2 * PARTS * pairs, owners * rows), BF16),
            pltpu.VMEM((2 * NFREQ, LAGS), BF16),
            pltpu.VMEM((2, 2 * PARTS * pairs, width // 2), F32),
            pltpu.VMEM((hours, channels * pairs, 2 * NFREQ), BF16),
            pltpu.VMEM((HALF_HOURS,) + share, F32),
            pltpu.SemaphoreType.DMA(()),
        ],
        compiler_params=pltpu.CompilerParams(vmem_limit_bytes=CORRELATE_VMEM),
    )(received, slots, lag_table())


def spread_kernel(*refs):
    part_refs, out_ref = refs[:-1], refs[-1]
    me = lax.axis_index("hour")
    for k, part_ref in enumerate(part_refs):
        out_ref[share_of(me ^ k)] = part_ref[...].astype(F32)


def swap(array, distance):
    return lax.ppermute(array, "hour", [(i, i ^ distance) for i in range(2 * HALF_HOURS)])


def stack_hours(shares, hours_all):
    mine = shares[0].astype(F32)
    for k in range(1, HALF_HOURS):
        mine = mine + swap(shares[k], k).astype(F32)
    mine = mine.astype(BF16)
    other = swap(mine, 2 * HALF_HOURS - 1)
    average = (mine.astype(F32) + other.astype(F32)) / hours_all
    size = jnp.abs(average) + 0.1
    stacked = (jnp.sign(average) * (size * size - 0.01)).astype(BF16)
    parts = [stacked] + [swap(stacked, k) for k in range(1, HALF_HOURS)]
    return pl.pallas_call(
        spread_kernel,
        out_shape=jax.ShapeDtypeStruct((HALF_HOURS,) + stacked.shape, F32),
        compiler_params=pltpu.CompilerParams(vmem_limit_bytes=SPREAD_VMEM),
        name="spread_result",
    )(*parts)


def local(raw_panels, window_start, valid_count, send_rows, pair_slots):
    hours = raw_panels.shape[1]
    pairs = pair_slots.shape[0]
    hour_devices = lax.axis_size("hour")
    panels = jnp.transpose(raw_panels, (1, 2, 0, 3))
    starts = jnp.transpose(window_start, (1, 2, 0))
    counts = jnp.transpose(valid_count, (1, 2, 0))
    outgoing = whiten(panels, starts, counts, jnp.transpose(send_rows[0]))
    received = lax.all_to_all(outgoing, "pair", split_axis=0, concat_axis=0, tiled=True)
    shares = correlate(received, jnp.transpose(pair_slots), hours)
    stacked = stack_hours(shares, hours * hour_devices)
    stacked = stacked.reshape(COMPS * COMPS, pairs, LAGS)
    return jnp.transpose(stacked, (1, 0, 2))


def solution(mesh):
    return jax.shard_map(
        local,
        mesh=mesh,
        in_specs=(
            P("pair", "hour", None, None),
            P("pair", "hour", None),
            P("pair", "hour", None),
            P("pair", None, None),
            P("pair", None),
        ),
        out_specs=P("pair", None, None),
        check_vma=False,
    )
```

```python
import functools
import math

import jax
import jax.numpy as jnp
import ml_dtypes
import numpy as np
from jax import lax
from jax.experimental import pallas as pl
from jax.experimental.pallas import tpu as pltpu
from jax.sharding import PartitionSpec as P

NFFT = 1024
NFREQ = 512
LAGS = 256
COMPS = 3
WINDOWS = 2
PARTS = 2 * WINDOWS
SMOOTH_HALF = 11
EPS_WHITE = 1e-06
HALF_HOURS = 4
WHITEN_VMEM = 58 * 2**20
CORRELATE_VMEM = 24 * 2**20
SPREAD_VMEM = 8 * 2**20
F32 = jnp.float32
BF16 = jnp.bfloat16


def dft_table():
    turns = np.outer(np.arange(NFFT), np.arange(NFREQ)) % NFFT
    angles = turns.astype(np.float32) * np.float32(2.0 * math.pi / NFFT)
    angles = angles.astype(np.float64)
    table = np.concatenate([np.cos(angles), -np.sin(angles)], axis=1)
    return table.astype(np.float32).astype(ml_dtypes.bfloat16)


def band_table():
    index = np.arange(NFREQ)
    band = np.abs(index[:, None] - index[None, :]) <= SMOOTH_HALF
    return band.astype(ml_dtypes.bfloat16)


def lag_table():
    turns = np.outer(np.arange(NFREQ), np.arange(LAGS) - LAGS // 2) % NFFT
    angles = turns.astype(np.float32) * np.float32(2.0 * math.pi / NFFT)
    angles = angles.astype(np.float64)
    weights = np.where(np.arange(NFREQ) == 0, 0.5, 1.0)[:, None]
    table = np.concatenate([weights * np.cos(angles), -weights * np.sin(angles)], axis=0)
    scale = 1.0 / math.sqrt(WINDOWS * NFREQ)
    return (table.astype(np.float32).astype(ml_dtypes.bfloat16) * scale).astype(ml_dtypes.bfloat16)


def column(row, size):
    here = lax.broadcasted_iota(jnp.int32, (size, size), 0)
    there = lax.broadcasted_iota(jnp.int32, (size, size), 1)
    spread = jnp.where(here == there, jnp.broadcast_to(row, (size, size)).astype(F32), 0.0)
    return jnp.sum(spread, axis=1, keepdims=True).astype(jnp.int32)


def cut(panel, start):
    stations, raw = panel.shape
    reach = raw - 2048
    bit = (start & 2048) != 0
    moved = jnp.where(bit, panel[:, 2048:], panel[:, :reach])
    samples = jnp.concatenate([moved, panel[:, reach : NFFT + 2048]], axis=1)
    for size in (1024, 512, 256, 128):
        bit = (start & size) != 0
        keep = NFFT + size
        samples = jnp.where(bit, samples[:, size : size + keep], samples[:, :keep])
    place = lax.broadcasted_iota(jnp.int32, (stations, 128), 1) + (start & 127)
    inside = place & 127
    turned = [
        jnp.take_along_axis(samples[:, t : t + 128], inside, axis=1, mode="promise_in_bounds")
        for t in range(0, NFFT + 128, 128)
    ]
    beyond = place >= 128
    return jnp.concatenate([jnp.where(beyond, turned[t + 1], turned[t]) for t in range(NFFT // 128)], axis=1)


def whiten_kernel(
    raw_hbm, start_hbm, count_hbm, send_hbm, dft_hbm, band_hbm, out_hbm,
    raw_ref, start_ref, count_ref, send_ref, dft_ref, band_ref, seg_ref, spec_ref, white_ref, pick_ref, out_ref,
    small_sem, raw_sem, table_sem, out_sem,
):
    hours, _, stations, _ = raw_ref.shape
    capacity, owners = send_ref.shape
    rows = capacity * PARTS
    block = COMPS * WINDOWS * stations
    small_copies = [
        pltpu.make_async_copy(start_hbm, start_ref, small_sem.at[0]),
        pltpu.make_async_copy(count_hbm, count_ref, small_sem.at[1]),
        pltpu.make_async_copy(send_hbm, send_ref, small_sem.at[2]),
    ]
    raw_copies = [pltpu.make_async_copy(raw_hbm.at[h], raw_ref.at[h], raw_sem.at[h]) for h in range(hours)]
    dft_copy = pltpu.make_async_copy(dft_hbm, dft_ref, table_sem.at[0])
    band_copy = pltpu.make_async_copy(band_hbm, band_ref, table_sem.at[1])
    for copy in small_copies + raw_copies:
        copy.start()
    dft_copy.start()
    band_copy.start()
    for copy in small_copies:
        copy.wait()

    out_row = lax.broadcasted_iota(jnp.int32, (owners * rows, owners), 0)
    owner = lax.broadcasted_iota(jnp.int32, (owners * rows, owners), 1)
    spread = (out_row // rows == owner).astype(BF16)
    wanted = lax.dot_general(
        spread, send_ref[...].astype(F32).astype(BF16), (((1,), (1,)), ((), ())), preferred_element_type=F32
    )
    out_row = lax.broadcasted_iota(jnp.int32, (owners * rows, capacity), 0)
    place = lax.broadcasted_iota(jnp.int32, (owners * rows, capacity), 1)
    wanted = jnp.sum(jnp.where(out_row % rows // PARTS == place, wanted, 0.0), axis=1, keepdims=True).astype(jnp.int32)
    out_row = lax.broadcasted_iota(jnp.int32, (owners * rows, PARTS * stations), 0)
    white_row = lax.broadcasted_iota(jnp.int32, (owners * rows, PARTS * stations), 1)
    pick_ref[...] = (out_row % PARTS * stations + wanted == white_row).astype(BF16)

    time = lax.broadcasted_iota(jnp.int32, (stations, NFFT), 1)
    for h in range(hours):
        raw_copies[h].wait()
        for w in range(WINDOWS):
            start = column(start_ref[h, w : w + 1, :], stations)
            count = column(count_ref[h, w : w + 1, :], stations)
            live = time < count
            share = count.astype(F32)
            for c in range(COMPS):
                piece = cut(raw_ref[h, c].astype(F32), start)
                piece = jnp.where(live, piece, 0.0)
                mean = jnp.sum(piece, axis=1, keepdims=True) / share
                row = h * block + (w * COMPS + c) * stations
                seg_ref[row : row + stations, :] = jnp.where(live, piece - mean, 0.0).astype(BF16)
    dft_copy.wait()
    band_copy.wait()
    out_copies = []
    spec_ref[...] = jnp.dot(seg_ref[...], dft_ref[...], preferred_element_type=F32)
    for h in range(hours):
        amps = []
        for w in range(WINDOWS):
            total = jnp.zeros((stations, NFREQ), F32)
            for c in range(COMPS):
                row = h * block + (w * COMPS + c) * stations
                real = spec_ref[row : row + stations, :NFREQ]
                imag = spec_ref[row : row + stations, NFREQ:]
                total = total + jnp.sqrt(real * real + imag * imag)
            amps.append(total)
        amp = jnp.concatenate(amps, axis=0)
        size = WINDOWS * stations
        high = amp.astype(BF16)
        rest = amp - high.astype(F32)
        middle = rest.astype(BF16)
        low = (rest - middle.astype(F32)).astype(BF16)
        sums = jnp.dot(jnp.concatenate([high, middle, low], axis=0), band_ref[...], preferred_element_type=F32)
        smooth = (sums[:size] + sums[size : 2 * size] + sums[2 * size :]) / (3.0 * (2 * SMOOTH_HALF + 1))
        inverse = 1.0 / (smooth + EPS_WHITE)
        for c in range(COMPS):
            cols = slice(c * NFREQ, (c + 1) * NFREQ)
            for w in range(WINDOWS):
                factor = inverse[w * stations : (w + 1) * stations]
                row = h * block + (w * COMPS + c) * stations
                for r in range(2):
                    part = spec_ref[row : row + stations, r * NFREQ : (r + 1) * NFREQ] * factor
                    to = (2 * w + r) * stations
                    white_ref[h, to : to + stations, cols] = part.astype(BF16)
            picked = jnp.dot(pick_ref[...], white_ref[h, :, cols], preferred_element_type=F32).astype(BF16)
            out_ref[h, :, :, cols] = picked.reshape(owners, rows, NFREQ)
        copy = pltpu.make_async_copy(out_ref.at[h], out_hbm.at[:, pl.ds(h * rows, rows), :], out_sem.at[h])
        copy.start()
        out_copies.append(copy)
    for copy in out_copies:
        copy.wait()


def share_of(device):
    return jnp.minimum(device, 2 * HALF_HOURS - 1 - device)


def correlate_kernel(recv_ref, slots_ref, lag_hbm, *refs):
    out_refs, (pick_ref, lag_ref, side_ref, cross_ref, total_ref, sem) = refs[:HALF_HOURS], refs[HALF_HOURS:]
    pairs = slots_ref.shape[1]
    owners, all_rows, _ = recv_ref.shape
    rows = all_rows // cross_ref.shape[0]
    half = NFREQ // 2
    lag_copy = pltpu.make_async_copy(lag_hbm, lag_ref, sem)
    lag_copy.start()

    arrived_row = lax.broadcasted_iota(jnp.int32, (pairs, owners * rows), 1)
    for side in range(2):
        first = column(slots_ref[side : side + 1, :], pairs) * PARTS
        for part in range(PARTS):
            row = (side * PARTS + part) * pairs
            pick_ref[row : row + pairs, :] = (first + part == arrived_row).astype(BF16)

    def select(h, n):
        for c in range(COMPS):
            col = c * NFREQ + n * half
            arrived = recv_ref[:, h * rows : (h + 1) * rows, col : col + half].reshape(owners * rows, half)
            side_ref[n, :, c * half : (c + 1) * half] = jnp.dot(pick_ref[...], arrived, preferred_element_type=F32)

    def cross(h, n):
        for k in range(0, pairs, 16):
            for f in range(0, half, 128):
                def load(side, part, comp):
                    row = (side * PARTS + part) * pairs + k
                    col = comp * half + f
                    return side_ref[n, row : row + 16, col : col + 128]
                left = [[load(0, part, comp) for comp in range(COMPS)] for part in range(PARTS)]
                right = [[load(1, part, comp) for comp in range(COMPS)] for part in range(PARTS)]
                for i in range(COMPS):
                    for j in range(COMPS):
                        real = left[0][i] * right[0][j] + left[2][i] * right[2][j]
                        real = real + (left[1][i] * right[1][j] + left[3][i] * right[3][j])
                        imag = left[1][i] * right[0][j] + left[3][i] * right[2][j]
                        imag = imag - (left[0][i] * right[1][j] + left[2][i] * right[3][j])
                        row = (COMPS * i + j) * pairs + k
                        col = n * half + f
                        cross_ref[h, row : row + 16, col : col + 128] = real.astype(BF16)
                        cross_ref[h, row : row + 16, NFREQ + col : NFREQ + col + 128] = imag.astype(BF16)

    def root(h):
        lagged = jnp.dot(cross_ref[h], lag_ref[...], preferred_element_type=F32)
        rooted = jnp.sqrt(jnp.abs(lagged) + 0.01) - 0.1
        rooted = jnp.where(lagged > 0.0, rooted, jnp.where(lagged < 0.0, -rooted, 0.0))
        rooted = rooted.reshape(total_ref.shape)
        if h == 0:
            total_ref[...] = rooted
        else:
            total_ref[...] += rooted

    lag_copy.wait()
    steps = [(h, n) for h in range(cross_ref.shape[0]) for n in range(2)]
    select(*steps[0])
    for now, later in zip(steps, steps[1:] + [None]):
        if later is not None:
            select(*later)
        cross(*now)
        if now[1] == 1:
            root(now[0])
    me = lax.axis_index("hour")
    for k, out_ref in enumerate(out_refs):
        out_ref[...] = total_ref[share_of(me ^ k)].astype(BF16)


def whiten(panels, starts, counts, send):
    hours, _, stations, raw = panels.shape
    capacity, owners = send.shape
    rows = capacity * PARTS
    width = COMPS * NFREQ
    block = WINDOWS * COMPS * stations
    hbm = pl.BlockSpec(memory_space=pltpu.HBM)
    return pl.pallas_call(
        whiten_kernel,
        in_specs=[hbm] * 6,
        out_specs=hbm,
        out_shape=jax.ShapeDtypeStruct((owners, hours * rows, width), BF16),
        scratch_shapes=[
            pltpu.VMEM(panels.shape, BF16),
            pltpu.VMEM(starts.shape, jnp.int32),
            pltpu.VMEM(counts.shape, jnp.int32),
            pltpu.VMEM(send.shape, jnp.int32),
            pltpu.VMEM((NFFT, 2 * NFREQ), BF16),
            pltpu.VMEM((NFREQ, NFREQ), BF16),
            pltpu.VMEM((hours * block, NFFT), BF16),
            pltpu.VMEM((hours * block, 2 * NFREQ), F32),
            pltpu.VMEM((hours, PARTS * stations, width), BF16),
            pltpu.VMEM((owners * rows, PARTS * stations), BF16),
            pltpu.VMEM((hours, owners, rows, width), BF16),
            pltpu.SemaphoreType.DMA((3,)),
            pltpu.SemaphoreType.DMA((hours,)),
            pltpu.SemaphoreType.DMA((2,)),
            pltpu.SemaphoreType.DMA((hours,)),
        ],
        compiler_params=pltpu.CompilerParams(vmem_limit_bytes=WHITEN_VMEM),
    )(panels, starts, counts, send, dft_table(), band_table())


def correlate(received, slots, hours):
    owners, all_rows, width = received.shape
    pairs = slots.shape[1]
    rows = all_rows // hours
    channels = COMPS * COMPS
    vmem = pl.BlockSpec(memory_space=pltpu.VMEM)
    share = (channels * pairs // HALF_HOURS, LAGS)
    return pl.pallas_call(
        correlate_kernel,
        in_specs=[vmem, vmem, pl.BlockSpec(memory_space=pltpu.HBM)],
        out_specs=[vmem] * HALF_HOURS,
        out_shape=[jax.ShapeDtypeStruct(share, BF16)] * HALF_HOURS,
        scratch_shapes=[
            pltpu.VMEM((2 * PARTS * pairs, owners * rows), BF16),
            pltpu.VMEM((2 * NFREQ, LAGS), BF16),
            pltpu.VMEM((2, 2 * PARTS * pairs, width // 2), F32),
            pltpu.VMEM((hours, channels * pairs, 2 * NFREQ), BF16),
            pltpu.VMEM((HALF_HOURS,) + share, F32),
            pltpu.SemaphoreType.DMA(()),
        ],
        compiler_params=pltpu.CompilerParams(vmem_limit_bytes=CORRELATE_VMEM),
    )(received, slots, lag_table())


def spread_kernel(*refs):
    part_refs, out_ref = refs[:-1], refs[-1]
    me = lax.axis_index("hour")
    for k, part_ref in enumerate(part_refs):
        out_ref[share_of(me ^ k)] = part_ref[...].astype(F32)


def swap(array, distance):
    return lax.ppermute(array, "hour", [(i, i ^ distance) for i in range(2 * HALF_HOURS)])


def stack_hours(shares, hours_all):
    mine = shares[0].astype(F32)
    for k in range(1, HALF_HOURS):
        mine = mine + swap(shares[k], k).astype(F32)
    mine = mine.astype(BF16)
    other = swap(mine, 2 * HALF_HOURS - 1)
    average = (mine.astype(F32) + other.astype(F32)) / hours_all
    size = jnp.abs(average) + 0.1
    stacked = (jnp.sign(average) * (size * size - 0.01)).astype(BF16)
    parts = [stacked] + [swap(stacked, k) for k in range(1, HALF_HOURS)]
    return pl.pallas_call(
        spread_kernel,
        out_shape=jax.ShapeDtypeStruct((HALF_HOURS,) + stacked.shape, F32),
        compiler_params=pltpu.CompilerParams(vmem_limit_bytes=SPREAD_VMEM),
        name="spread_result",
    )(*parts)


def local(raw_panels, window_start, valid_count, send_rows, pair_slots):
    hours = raw_panels.shape[1]
    pairs = pair_slots.shape[0]
    hour_devices = lax.axis_size("hour")
    panels = jnp.transpose(raw_panels, (1, 2, 0, 3))
    starts = jnp.transpose(window_start, (1, 2, 0))
    counts = jnp.transpose(valid_count, (1, 2, 0))
    outgoing = whiten(panels, starts, counts, jnp.transpose(send_rows[0]))
    received = lax.all_to_all(outgoing, "pair", split_axis=0, concat_axis=0, tiled=True)
    shares = correlate(received, jnp.transpose(pair_slots), hours)
    stacked = stack_hours(shares, hours * hour_devices)
    stacked = stacked.reshape(COMPS * COMPS, pairs, LAGS)
    return jnp.transpose(stacked, (1, 0, 2))


def solution(mesh):
    return jax.shard_map(
        local,
        mesh=mesh,
        in_specs=(
            P("pair", "hour", None, None),
            P("pair", "hour", None),
            P("pair", "hour", None),
            P("pair", None, None),
            P("pair", None),
        ),
        out_specs=P("pair", None, None),
        check_vma=False,
    )
```

```python
import functools
import math

import jax
import jax.numpy as jnp
import ml_dtypes
import numpy as np
from jax import lax
from jax.experimental import pallas as pl
from jax.experimental.pallas import tpu as pltpu
from jax.sharding import PartitionSpec as P

NFFT = 1024
NFREQ = 512
LAGS = 256
COMPS = 3
WINDOWS = 2
PARTS = 2 * WINDOWS
SMOOTH_HALF = 11
EPS_WHITE = 1e-06
HALF_HOURS = 4
PARTNER = 6
WHITEN_VMEM = 58 * 2**20
CORRELATE_VMEM = 24 * 2**20
SPREAD_VMEM = 8 * 2**20
F32 = jnp.float32
BF16 = jnp.bfloat16


def dft_table():
    turns = np.outer(np.arange(NFFT), np.arange(NFREQ)) % NFFT
    angles = turns.astype(np.float32) * np.float32(2.0 * math.pi / NFFT)
    angles = angles.astype(np.float64)
    table = np.concatenate([np.cos(angles), -np.sin(angles)], axis=1)
    return table.astype(np.float32).astype(ml_dtypes.bfloat16)


def band_table():
    index = np.arange(NFREQ)
    band = np.abs(index[:, None] - index[None, :]) <= SMOOTH_HALF
    return band.astype(ml_dtypes.bfloat16)


def lag_table():
    turns = np.outer(np.arange(NFREQ), np.arange(LAGS) - LAGS // 2) % NFFT
    angles = turns.astype(np.float32) * np.float32(2.0 * math.pi / NFFT)
    angles = angles.astype(np.float64)
    weights = np.where(np.arange(NFREQ) == 0, 0.5, 1.0)[:, None]
    table = np.concatenate([weights * np.cos(angles), -weights * np.sin(angles)], axis=0)
    scale = 1.0 / math.sqrt(WINDOWS * NFREQ)
    return (table.astype(np.float32).astype(ml_dtypes.bfloat16) * scale).astype(ml_dtypes.bfloat16)


def column(row, size):
    here = lax.broadcasted_iota(jnp.int32, (size, size), 0)
    there = lax.broadcasted_iota(jnp.int32, (size, size), 1)
    spread = jnp.where(here == there, jnp.broadcast_to(row, (size, size)).astype(F32), 0.0)
    return jnp.sum(spread, axis=1, keepdims=True).astype(jnp.int32)


def cut(panel, start):
    stations, raw = panel.shape
    reach = raw - 2048
    bit = (start & 2048) != 0
    moved = jnp.where(bit, panel[:, 2048:], panel[:, :reach])
    samples = jnp.concatenate([moved, panel[:, reach : NFFT + 2048]], axis=1)
    for size in (1024, 512, 256, 128):
        bit = (start & size) != 0
        keep = NFFT + size
        samples = jnp.where(bit, samples[:, size : size + keep], samples[:, :keep])
    place = lax.broadcasted_iota(jnp.int32, (stations, 128), 1) + (start & 127)
    inside = place & 127
    turned = [
        jnp.take_along_axis(samples[:, t : t + 128], inside, axis=1, mode="promise_in_bounds")
        for t in range(0, NFFT + 128, 128)
    ]
    beyond = place >= 128
    return jnp.concatenate([jnp.where(beyond, turned[t + 1], turned[t]) for t in range(NFFT // 128)], axis=1)


def whiten_kernel(
    raw_hbm, start_hbm, count_hbm, send_hbm, dft_hbm, band_hbm, out_hbm,
    raw_ref, start_ref, count_ref, send_ref, dft_ref, band_ref, seg_ref, spec_ref, white_ref, pick_ref, out_ref,
    small_sem, raw_sem, table_sem, out_sem,
):
    hours, _, stations, _ = raw_ref.shape
    capacity, owners = send_ref.shape
    rows = capacity * PARTS
    block = COMPS * WINDOWS * stations
    small_copies = [
        pltpu.make_async_copy(start_hbm, start_ref, small_sem.at[0]),
        pltpu.make_async_copy(count_hbm, count_ref, small_sem.at[1]),
        pltpu.make_async_copy(send_hbm, send_ref, small_sem.at[2]),
    ]
    raw_copies = [pltpu.make_async_copy(raw_hbm.at[h], raw_ref.at[h], raw_sem.at[h]) for h in range(hours)]
    dft_copy = pltpu.make_async_copy(dft_hbm, dft_ref, table_sem.at[0])
    band_copy = pltpu.make_async_copy(band_hbm, band_ref, table_sem.at[1])
    for copy in small_copies + raw_copies:
        copy.start()
    dft_copy.start()
    band_copy.start()
    for copy in small_copies:
        copy.wait()

    out_row = lax.broadcasted_iota(jnp.int32, (owners * rows, owners), 0)
    owner = lax.broadcasted_iota(jnp.int32, (owners * rows, owners), 1)
    spread = (out_row // rows == owner).astype(BF16)
    wanted = lax.dot_general(
        spread, send_ref[...].astype(F32).astype(BF16), (((1,), (1,)), ((), ())), preferred_element_type=F32
    )
    out_row = lax.broadcasted_iota(jnp.int32, (owners * rows, capacity), 0)
    place = lax.broadcasted_iota(jnp.int32, (owners * rows, capacity), 1)
    wanted = jnp.sum(jnp.where(out_row % rows // PARTS == place, wanted, 0.0), axis=1, keepdims=True).astype(jnp.int32)
    out_row = lax.broadcasted_iota(jnp.int32, (owners * rows, PARTS * stations), 0)
    white_row = lax.broadcasted_iota(jnp.int32, (owners * rows, PARTS * stations), 1)
    pick_ref[...] = (out_row % PARTS * stations + wanted == white_row).astype(BF16)

    time = lax.broadcasted_iota(jnp.int32, (stations, NFFT), 1)
    out_copies = []

    def cut_hour(h):
        raw_copies[h].wait()
        for w in range(WINDOWS):
            start = column(start_ref[h, w : w + 1, :], stations)
            count = column(count_ref[h, w : w + 1, :], stations)
            live = time < count
            share = count.astype(F32)
            for c in range(COMPS):
                piece = cut(raw_ref[h, c].astype(F32), start)
                piece = jnp.where(live, piece, 0.0)
                mean = jnp.sum(piece, axis=1, keepdims=True) / share
                row = h * block + (w * COMPS + c) * stations
                seg_ref[row : row + stations, :] = jnp.where(live, piece - mean, 0.0).astype(BF16)

    def send_hour(h):
        here = slice(h * block, (h + 1) * block)
        spec_ref[here, :] = jnp.dot(seg_ref[here, :], dft_ref[...], preferred_element_type=F32)
        amps = []
        for w in range(WINDOWS):
            total = jnp.zeros((stations, NFREQ), F32)
            for c in range(COMPS):
                row = h * block + (w * COMPS + c) * stations
                real = spec_ref[row : row + stations, :NFREQ]
                imag = spec_ref[row : row + stations, NFREQ:]
                total = total + jnp.sqrt(real * real + imag * imag)
            amps.append(total)
        amp = jnp.concatenate(amps, axis=0)
        size = WINDOWS * stations
        high = amp.astype(BF16)
        rest = amp - high.astype(F32)
        middle = rest.astype(BF16)
        low = (rest - middle.astype(F32)).astype(BF16)
        sums = jnp.dot(jnp.concatenate([high, middle, low], axis=0), band_ref[...], preferred_element_type=F32)
        smooth = (sums[:size] + sums[size : 2 * size] + sums[2 * size :]) / (3.0 * (2 * SMOOTH_HALF + 1))
        inverse = 1.0 / (smooth + EPS_WHITE)
        for c in range(COMPS):
            cols = slice(c * NFREQ, (c + 1) * NFREQ)
            for w in range(WINDOWS):
                factor = inverse[w * stations : (w + 1) * stations]
                row = h * block + (w * COMPS + c) * stations
                for r in range(2):
                    part = spec_ref[row : row + stations, r * NFREQ : (r + 1) * NFREQ] * factor
                    to = (2 * w + r) * stations
                    white_ref[h, to : to + stations, cols] = part.astype(BF16)
            picked = jnp.dot(pick_ref[...], white_ref[h, :, cols], preferred_element_type=F32).astype(BF16)
            out_ref[h, :, :, cols] = picked.reshape(owners, rows, NFREQ)
        copy = pltpu.make_async_copy(out_ref.at[h], out_hbm.at[:, pl.ds(h * rows, rows), :], out_sem.at[h])
        copy.start()
        out_copies.append(copy)

    cut_hour(0)
    dft_copy.wait()
    band_copy.wait()
    for h in range(hours):
        if h + 1 < hours:
            cut_hour(h + 1)
        send_hour(h)
    for copy in out_copies:
        copy.wait()


def share_of(device):
    return jnp.where(device < HALF_HOURS, device, device ^ PARTNER)


def correlate_kernel(recv_ref, slots_ref, lag_hbm, *refs):
    out_refs, (pick_ref, lag_ref, side_ref, cross_ref, total_ref, sem) = refs[:HALF_HOURS], refs[HALF_HOURS:]
    pairs = slots_ref.shape[1]
    owners, all_rows, _ = recv_ref.shape
    rows = all_rows // cross_ref.shape[0]
    half = NFREQ // 2
    lag_copy = pltpu.make_async_copy(lag_hbm, lag_ref, sem)
    lag_copy.start()

    arrived_row = lax.broadcasted_iota(jnp.int32, (pairs, owners * rows), 1)
    for side in range(2):
        first = column(slots_ref[side : side + 1, :], pairs) * PARTS
        for part in range(PARTS):
            row = (side * PARTS + part) * pairs
            pick_ref[row : row + pairs, :] = (first + part == arrived_row).astype(BF16)

    def select(h, n):
        for c in range(COMPS):
            col = c * NFREQ + n * half
            arrived = recv_ref[:, h * rows : (h + 1) * rows, col : col + half].reshape(owners * rows, half)
            side_ref[n, :, c * half : (c + 1) * half] = jnp.dot(pick_ref[...], arrived, preferred_element_type=F32)

    def cross(h, n):
        for k in range(0, pairs, 16):
            for f in range(0, half, 128):
                def load(side, part, comp):
                    row = (side * PARTS + part) * pairs + k
                    col = comp * half + f
                    return side_ref[n, row : row + 16, col : col + 128]
                left = [[load(0, part, comp) for comp in range(COMPS)] for part in range(PARTS)]
                right = [[load(1, part, comp) for comp in range(COMPS)] for part in range(PARTS)]
                for i in range(COMPS):
                    for j in range(COMPS):
                        real = left[0][i] * right[0][j] + left[2][i] * right[2][j]
                        real = real + (left[1][i] * right[1][j] + left[3][i] * right[3][j])
                        imag = left[1][i] * right[0][j] + left[3][i] * right[2][j]
                        imag = imag - (left[0][i] * right[1][j] + left[2][i] * right[3][j])
                        row = (COMPS * i + j) * pairs + k
                        col = n * half + f
                        cross_ref[h, row : row + 16, col : col + 128] = real.astype(BF16)
                        cross_ref[h, row : row + 16, NFREQ + col : NFREQ + col + 128] = imag.astype(BF16)

    def root(h):
        lagged = jnp.dot(cross_ref[h], lag_ref[...], preferred_element_type=F32)
        size = jnp.abs(lagged) + 0.01
        rooted = size * lax.rsqrt(size) - 0.1
        rooted = jnp.where(lagged < 0.0, -rooted, rooted)
        rooted = rooted.reshape(total_ref.shape)
        if h == 0:
            total_ref[...] = rooted
        else:
            total_ref[...] += rooted

    lag_copy.wait()
    steps = [(h, n) for h in range(cross_ref.shape[0]) for n in range(2)]
    select(*steps[0])
    for now, later in zip(steps, steps[1:] + [None]):
        if later is not None:
            select(*later)
        cross(*now)
        if now[1] == 1:
            root(now[0])
    me = lax.axis_index("hour")
    for k, out_ref in enumerate(out_refs):
        out_ref[...] = total_ref[share_of(me ^ k)].astype(BF16)


def whiten(panels, starts, counts, send):
    hours, _, stations, raw = panels.shape
    capacity, owners = send.shape
    rows = capacity * PARTS
    width = COMPS * NFREQ
    block = WINDOWS * COMPS * stations
    hbm = pl.BlockSpec(memory_space=pltpu.HBM)
    return pl.pallas_call(
        whiten_kernel,
        in_specs=[hbm] * 6,
        out_specs=hbm,
        out_shape=jax.ShapeDtypeStruct((owners, hours * rows, width), BF16),
        scratch_shapes=[
            pltpu.VMEM(panels.shape, BF16),
            pltpu.VMEM(starts.shape, jnp.int32),
            pltpu.VMEM(counts.shape, jnp.int32),
            pltpu.VMEM(send.shape, jnp.int32),
            pltpu.VMEM((NFFT, 2 * NFREQ), BF16),
            pltpu.VMEM((NFREQ, NFREQ), BF16),
            pltpu.VMEM((hours * block, NFFT), BF16),
            pltpu.VMEM((hours * block, 2 * NFREQ), F32),
            pltpu.VMEM((hours, PARTS * stations, width), BF16),
            pltpu.VMEM((owners * rows, PARTS * stations), BF16),
            pltpu.VMEM((hours, owners, rows, width), BF16),
            pltpu.SemaphoreType.DMA((3,)),
            pltpu.SemaphoreType.DMA((hours,)),
            pltpu.SemaphoreType.DMA((2,)),
            pltpu.SemaphoreType.DMA((hours,)),
        ],
        compiler_params=pltpu.CompilerParams(vmem_limit_bytes=WHITEN_VMEM),
    )(panels, starts, counts, send, dft_table(), band_table())


def correlate(received, slots, hours):
    owners, all_rows, width = received.shape
    pairs = slots.shape[1]
    rows = all_rows // hours
    channels = COMPS * COMPS
    vmem = pl.BlockSpec(memory_space=pltpu.VMEM)
    share = (channels * pairs // HALF_HOURS, LAGS)
    return pl.pallas_call(
        correlate_kernel,
        in_specs=[vmem, vmem, pl.BlockSpec(memory_space=pltpu.HBM)],
        out_specs=[vmem] * HALF_HOURS,
        out_shape=[jax.ShapeDtypeStruct(share, BF16)] * HALF_HOURS,
        scratch_shapes=[
            pltpu.VMEM((2 * PARTS * pairs, owners * rows), BF16),
            pltpu.VMEM((2 * NFREQ, LAGS), BF16),
            pltpu.VMEM((2, 2 * PARTS * pairs, width // 2), F32),
            pltpu.VMEM((hours, channels * pairs, 2 * NFREQ), BF16),
            pltpu.VMEM((HALF_HOURS,) + share, F32),
            pltpu.SemaphoreType.DMA(()),
        ],
        compiler_params=pltpu.CompilerParams(vmem_limit_bytes=CORRELATE_VMEM),
    )(received, slots, lag_table())


def spread_kernel(*refs):
    part_refs, out_ref = refs[:-1], refs[-1]
    me = lax.axis_index("hour")
    for k, part_ref in enumerate(part_refs):
        out_ref[share_of(me ^ k)] = part_ref[...].astype(F32)


def swap(array, distance):
    return lax.ppermute(array, "hour", [(i, i ^ distance) for i in range(2 * HALF_HOURS)])


def stack_hours(shares, hours_all):
    mine = shares[0].astype(F32)
    for k in range(1, HALF_HOURS):
        mine = mine + swap(shares[k], k).astype(F32)
    mine = mine.astype(BF16)
    other = swap(mine, PARTNER)
    average = (mine.astype(F32) + other.astype(F32)) / hours_all
    size = jnp.abs(average) + 0.1
    stacked = (jnp.sign(average) * (size * size - 0.01)).astype(BF16)
    parts = [stacked] + [swap(stacked, k) for k in range(1, HALF_HOURS)]
    return pl.pallas_call(
        spread_kernel,
        out_shape=jax.ShapeDtypeStruct((HALF_HOURS,) + stacked.shape, F32),
        compiler_params=pltpu.CompilerParams(vmem_limit_bytes=SPREAD_VMEM),
        name="spread_result",
    )(*parts)


def local(raw_panels, window_start, valid_count, send_rows, pair_slots):
    hours = raw_panels.shape[1]
    pairs = pair_slots.shape[0]
    hour_devices = lax.axis_size("hour")
    panels = jnp.transpose(raw_panels, (1, 2, 0, 3))
    starts = jnp.transpose(window_start, (1, 2, 0))
    counts = jnp.transpose(valid_count, (1, 2, 0))
    outgoing = whiten(panels, starts, counts, jnp.transpose(send_rows[0]))
    received = lax.all_to_all(outgoing, "pair", split_axis=0, concat_axis=0, tiled=True)
    shares = correlate(received, jnp.transpose(pair_slots), hours)
    stacked = stack_hours(shares, hours * hour_devices)
    stacked = stacked.reshape(COMPS * COMPS, pairs, LAGS)
    return jnp.transpose(stacked, (1, 0, 2))


def solution(mesh):
    return jax.shard_map(
        local,
        mesh=mesh,
        in_specs=(
            P("pair", "hour", None, None),
            P("pair", "hour", None),
            P("pair", "hour", None),
            P("pair", None, None),
            P("pair", None),
        ),
        out_specs=P("pair", None, None),
        check_vma=False,
    )
```

```python
import functools
import math

import jax
import jax.numpy as jnp
import ml_dtypes
import numpy as np
from jax import lax
from jax.experimental import pallas as pl
from jax.experimental.pallas import tpu as pltpu
from jax.sharding import PartitionSpec as P

NFFT = 1024
NFREQ = 512
LAGS = 256
COMPS = 3
WINDOWS = 2
PARTS = 2 * WINDOWS
SMOOTH_HALF = 11
EPS_WHITE = 1e-06
HALF_HOURS = 4
WHITEN_VMEM = 58 * 2**20
CORRELATE_VMEM = 24 * 2**20
SPREAD_VMEM = 8 * 2**20
F32 = jnp.float32
BF16 = jnp.bfloat16


def dft_table():
    turns = np.outer(np.arange(NFFT), np.arange(NFREQ)) % NFFT
    angles = turns.astype(np.float32) * np.float32(2.0 * math.pi / NFFT)
    angles = angles.astype(np.float64)
    table = np.concatenate([np.cos(angles), -np.sin(angles)], axis=1)
    return table.astype(np.float32).astype(ml_dtypes.bfloat16)


def band_table():
    index = np.arange(NFREQ)
    band = np.abs(index[:, None] - index[None, :]) <= SMOOTH_HALF
    return band.astype(ml_dtypes.bfloat16)


def lag_table():
    turns = np.outer(np.arange(NFREQ), np.arange(LAGS) - LAGS // 2) % NFFT
    angles = turns.astype(np.float32) * np.float32(2.0 * math.pi / NFFT)
    angles = angles.astype(np.float64)
    weights = np.where(np.arange(NFREQ) == 0, 0.5, 1.0)[:, None]
    table = np.concatenate([weights * np.cos(angles), -weights * np.sin(angles)], axis=0)
    scale = 1.0 / math.sqrt(WINDOWS * NFREQ)
    return (table.astype(np.float32).astype(ml_dtypes.bfloat16) * scale).astype(ml_dtypes.bfloat16)


def column(row, size):
    here = lax.broadcasted_iota(jnp.int32, (size, size), 0)
    there = lax.broadcasted_iota(jnp.int32, (size, size), 1)
    spread = jnp.where(here == there, jnp.broadcast_to(row, (size, size)).astype(F32), 0.0)
    return jnp.sum(spread, axis=1, keepdims=True).astype(jnp.int32)


def cut(panel, start):
    stations, raw = panel.shape
    reach = raw - 2048
    bit = (start & 2048) != 0
    moved = jnp.where(bit, panel[:, 2048:], panel[:, :reach])
    samples = jnp.concatenate([moved, panel[:, reach : NFFT + 2048]], axis=1)
    for size in (1024, 512, 256, 128):
        bit = (start & size) != 0
        keep = NFFT + size
        samples = jnp.where(bit, samples[:, size : size + keep], samples[:, :keep])
    place = lax.broadcasted_iota(jnp.int32, (stations, 128), 1) + (start & 127)
    inside = place & 127
    turned = [
        jnp.take_along_axis(samples[:, t : t + 128], inside, axis=1, mode="promise_in_bounds")
        for t in range(0, NFFT + 128, 128)
    ]
    beyond = place >= 128
    return jnp.concatenate([jnp.where(beyond, turned[t + 1], turned[t]) for t in range(NFFT // 128)], axis=1)


def whiten_kernel(
    raw_hbm, start_hbm, count_hbm, send_hbm, dft_hbm, band_hbm, out_hbm,
    raw_ref, start_ref, count_ref, send_ref, dft_ref, band_ref, seg_ref, spec_ref, white_ref, pick_ref, out_ref,
    small_sem, raw_sem, table_sem, out_sem,
):
    hours, _, stations, _ = raw_ref.shape
    capacity, owners = send_ref.shape
    rows = capacity * PARTS
    block = COMPS * WINDOWS * stations
    small_copies = [
        pltpu.make_async_copy(start_hbm, start_ref, small_sem.at[0]),
        pltpu.make_async_copy(count_hbm, count_ref, small_sem.at[1]),
        pltpu.make_async_copy(send_hbm, send_ref, small_sem.at[2]),
    ]
    raw_copies = [pltpu.make_async_copy(raw_hbm.at[h], raw_ref.at[h], raw_sem.at[h]) for h in range(hours)]
    dft_copy = pltpu.make_async_copy(dft_hbm, dft_ref, table_sem.at[0])
    band_copy = pltpu.make_async_copy(band_hbm, band_ref, table_sem.at[1])
    for copy in small_copies + raw_copies:
        copy.start()
    dft_copy.start()
    band_copy.start()
    for copy in small_copies:
        copy.wait()

    out_row = lax.broadcasted_iota(jnp.int32, (owners * rows, owners), 0)
    owner = lax.broadcasted_iota(jnp.int32, (owners * rows, owners), 1)
    spread = (out_row // rows == owner).astype(BF16)
    wanted = lax.dot_general(
        spread, send_ref[...].astype(F32).astype(BF16), (((1,), (1,)), ((), ())), preferred_element_type=F32
    )
    out_row = lax.broadcasted_iota(jnp.int32, (owners * rows, capacity), 0)
    place = lax.broadcasted_iota(jnp.int32, (owners * rows, capacity), 1)
    wanted = jnp.sum(jnp.where(out_row % rows // PARTS == place, wanted, 0.0), axis=1, keepdims=True).astype(jnp.int32)
    out_row = lax.broadcasted_iota(jnp.int32, (owners * rows, PARTS * stations), 0)
    white_row = lax.broadcasted_iota(jnp.int32, (owners * rows, PARTS * stations), 1)
    pick_ref[...] = (out_row % PARTS * stations + wanted == white_row).astype(BF16)

    time = lax.broadcasted_iota(jnp.int32, (stations, NFFT), 1)
    out_copies = []

    def cut_hour(h):
        raw_copies[h].wait()
        for w in range(WINDOWS):
            start = column(start_ref[h, w : w + 1, :], stations)
            count = column(count_ref[h, w : w + 1, :], stations)
            live = time < count
            share = count.astype(F32)
            for c in range(COMPS):
                piece = cut(raw_ref[h, c].astype(F32), start)
                piece = jnp.where(live, piece, 0.0)
                mean = jnp.sum(piece, axis=1, keepdims=True) / share
                row = h * block + (w * COMPS + c) * stations
                seg_ref[row : row + stations, :] = jnp.where(live, piece - mean, 0.0).astype(BF16)

    def send_hour(h):
        here = slice(h * block, (h + 1) * block)
        spec_ref[here, :] = jnp.dot(seg_ref[here, :], dft_ref[...], preferred_element_type=F32)
        amps = []
        for w in range(WINDOWS):
            total = jnp.zeros((stations, NFREQ), F32)
            for c in range(COMPS):
                row = h * block + (w * COMPS + c) * stations
                real = spec_ref[row : row + stations, :NFREQ]
                imag = spec_ref[row : row + stations, NFREQ:]
                total = total + jnp.sqrt(real * real + imag * imag)
            amps.append(total)
        amp = jnp.concatenate(amps, axis=0)
        size = WINDOWS * stations
        high = amp.astype(BF16)
        rest = amp - high.astype(F32)
        middle = rest.astype(BF16)
        low = (rest - middle.astype(F32)).astype(BF16)
        sums = jnp.dot(jnp.concatenate([high, middle, low], axis=0), band_ref[...], preferred_element_type=F32)
        smooth = (sums[:size] + sums[size : 2 * size] + sums[2 * size :]) / (3.0 * (2 * SMOOTH_HALF + 1))
        inverse = 1.0 / (smooth + EPS_WHITE)
        for c in range(COMPS):
            cols = slice(c * NFREQ, (c + 1) * NFREQ)
            for w in range(WINDOWS):
                factor = inverse[w * stations : (w + 1) * stations]
                row = h * block + (w * COMPS + c) * stations
                for r in range(2):
                    part = spec_ref[row : row + stations, r * NFREQ : (r + 1) * NFREQ] * factor
                    to = (2 * w + r) * stations
                    white_ref[h, to : to + stations, cols] = part.astype(BF16)
            picked = jnp.dot(pick_ref[...], white_ref[h, :, cols], preferred_element_type=F32).astype(BF16)
            out_ref[h, :, :, cols] = picked.reshape(owners, rows, NFREQ)
        copy = pltpu.make_async_copy(out_ref.at[h], out_hbm.at[:, pl.ds(h * rows, rows), :], out_sem.at[h])
        copy.start()
        out_copies.append(copy)

    cut_hour(0)
    dft_copy.wait()
    band_copy.wait()
    for h in range(hours):
        if h + 1 < hours:
            cut_hour(h + 1)
        send_hour(h)
    for copy in out_copies:
        copy.wait()


def share_of(device):
    return jnp.minimum(device, 2 * HALF_HOURS - 1 - device)


def correlate_kernel(recv_ref, slots_ref, lag_hbm, *refs):
    out_refs, (pick_ref, lag_ref, side_ref, cross_ref, total_ref, sem) = refs[:HALF_HOURS], refs[HALF_HOURS:]
    pairs = slots_ref.shape[1]
    owners, all_rows, _ = recv_ref.shape
    rows = all_rows // cross_ref.shape[0]
    half = NFREQ // 2
    lag_copy = pltpu.make_async_copy(lag_hbm, lag_ref, sem)
    lag_copy.start()

    arrived_row = lax.broadcasted_iota(jnp.int32, (pairs, owners * rows), 1)
    for side in range(2):
        first = column(slots_ref[side : side + 1, :], pairs) * PARTS
        for part in range(PARTS):
            row = (side * PARTS + part) * pairs
            pick_ref[row : row + pairs, :] = (first + part == arrived_row).astype(BF16)

    def select(h, n):
        for c in range(COMPS):
            col = c * NFREQ + n * half
            arrived = recv_ref[:, h * rows : (h + 1) * rows, col : col + half].reshape(owners * rows, half)
            side_ref[n, :, c * half : (c + 1) * half] = jnp.dot(pick_ref[...], arrived, preferred_element_type=F32)

    def cross(h, n):
        for k in range(0, pairs, 16):
            for f in range(0, half, 128):
                def load(side, part, comp):
                    row = (side * PARTS + part) * pairs + k
                    col = comp * half + f
                    return side_ref[n, row : row + 16, col : col + 128]
                left = [[load(0, part, comp) for comp in range(COMPS)] for part in range(PARTS)]
                right = [[load(1, part, comp) for comp in range(COMPS)] for part in range(PARTS)]
                for i in range(COMPS):
                    for j in range(COMPS):
                        real = left[0][i] * right[0][j] + left[2][i] * right[2][j]
                        real = real + (left[1][i] * right[1][j] + left[3][i] * right[3][j])
                        imag = left[1][i] * right[0][j] + left[3][i] * right[2][j]
                        imag = imag - (left[0][i] * right[1][j] + left[2][i] * right[3][j])
                        row = (COMPS * i + j) * pairs + k
                        col = n * half + f
                        cross_ref[h, row : row + 16, col : col + 128] = real.astype(BF16)
                        cross_ref[h, row : row + 16, NFREQ + col : NFREQ + col + 128] = imag.astype(BF16)

    def root(h):
        lagged = jnp.dot(cross_ref[h], lag_ref[...], preferred_element_type=F32)
        size = jnp.abs(lagged) + 0.01
        rooted = size * lax.rsqrt(size) - 0.1
        rooted = jnp.where(lagged < 0.0, -rooted, rooted)
        rooted = rooted.reshape(total_ref.shape)
        if h == 0:
            total_ref[...] = rooted
        else:
            total_ref[...] += rooted

    lag_copy.wait()
    steps = [(h, n) for h in range(cross_ref.shape[0]) for n in range(2)]
    select(*steps[0])
    for now, later in zip(steps, steps[1:] + [None]):
        if later is not None:
            select(*later)
        cross(*now)
        if now[1] == 1:
            root(now[0])
    me = lax.axis_index("hour")
    for k, out_ref in enumerate(out_refs):
        out_ref[...] = total_ref[share_of(me ^ k)].astype(BF16)


def whiten(panels, starts, counts, send):
    hours, _, stations, raw = panels.shape
    capacity, owners = send.shape
    rows = capacity * PARTS
    width = COMPS * NFREQ
    block = WINDOWS * COMPS * stations
    hbm = pl.BlockSpec(memory_space=pltpu.HBM)
    return pl.pallas_call(
        whiten_kernel,
        in_specs=[hbm] * 6,
        out_specs=hbm,
        out_shape=jax.ShapeDtypeStruct((owners, hours * rows, width), BF16),
        scratch_shapes=[
            pltpu.VMEM(panels.shape, BF16),
            pltpu.VMEM(starts.shape, jnp.int32),
            pltpu.VMEM(counts.shape, jnp.int32),
            pltpu.VMEM(send.shape, jnp.int32),
            pltpu.VMEM((NFFT, 2 * NFREQ), BF16),
            pltpu.VMEM((NFREQ, NFREQ), BF16),
            pltpu.VMEM((hours * block, NFFT), BF16),
            pltpu.VMEM((hours * block, 2 * NFREQ), F32),
            pltpu.VMEM((hours, PARTS * stations, width), BF16),
            pltpu.VMEM((owners * rows, PARTS * stations), BF16),
            pltpu.VMEM((hours, owners, rows, width), BF16),
            pltpu.SemaphoreType.DMA((3,)),
            pltpu.SemaphoreType.DMA((hours,)),
            pltpu.SemaphoreType.DMA((2,)),
            pltpu.SemaphoreType.DMA((hours,)),
        ],
        compiler_params=pltpu.CompilerParams(vmem_limit_bytes=WHITEN_VMEM),
    )(panels, starts, counts, send, dft_table(), band_table())


def correlate(received, slots, hours):
    owners, all_rows, width = received.shape
    pairs = slots.shape[1]
    rows = all_rows // hours
    channels = COMPS * COMPS
    vmem = pl.BlockSpec(memory_space=pltpu.VMEM)
    share = (channels * pairs // HALF_HOURS, LAGS)
    return pl.pallas_call(
        correlate_kernel,
        in_specs=[vmem, vmem, pl.BlockSpec(memory_space=pltpu.HBM)],
        out_specs=[vmem] * HALF_HOURS,
        out_shape=[jax.ShapeDtypeStruct(share, BF16)] * HALF_HOURS,
        scratch_shapes=[
            pltpu.VMEM((2 * PARTS * pairs, owners * rows), BF16),
            pltpu.VMEM((2 * NFREQ, LAGS), BF16),
            pltpu.VMEM((2, 2 * PARTS * pairs, width // 2), F32),
            pltpu.VMEM((hours, channels * pairs, 2 * NFREQ), BF16),
            pltpu.VMEM((HALF_HOURS,) + share, F32),
            pltpu.SemaphoreType.DMA(()),
        ],
        compiler_params=pltpu.CompilerParams(vmem_limit_bytes=CORRELATE_VMEM),
    )(received, slots, lag_table())


def spread_kernel(*refs):
    part_refs, out_ref = refs[:-1], refs[-1]
    me = lax.axis_index("hour")
    for k, part_ref in enumerate(part_refs):
        out_ref[share_of(me ^ k)] = part_ref[...].astype(F32)


def swap(array, distance):
    return lax.ppermute(array, "hour", [(i, i ^ distance) for i in range(2 * HALF_HOURS)])


def stack_hours(shares, hours_all):
    mine = shares[0].astype(F32)
    for k in range(1, HALF_HOURS):
        mine = mine + swap(shares[k], k).astype(F32)
    mine = mine.astype(BF16)
    other = swap(mine, 2 * HALF_HOURS - 1)
    average = (mine.astype(F32) + other.astype(F32)) / hours_all
    size = jnp.abs(average) + 0.1
    stacked = (jnp.sign(average) * (size * size - 0.01)).astype(BF16)
    parts = [stacked] + [swap(stacked, k) for k in range(1, HALF_HOURS)]
    return pl.pallas_call(
        spread_kernel,
        out_shape=jax.ShapeDtypeStruct((HALF_HOURS,) + stacked.shape, F32),
        compiler_params=pltpu.CompilerParams(vmem_limit_bytes=SPREAD_VMEM),
        name="spread_result",
    )(*parts)


def local(raw_panels, window_start, valid_count, send_rows, pair_slots):
    hours = raw_panels.shape[1]
    pairs = pair_slots.shape[0]
    hour_devices = lax.axis_size("hour")
    panels = jnp.transpose(raw_panels, (1, 2, 0, 3))
    starts = jnp.transpose(window_start, (1, 2, 0))
    counts = jnp.transpose(valid_count, (1, 2, 0))
    outgoing = whiten(panels, starts, counts, jnp.transpose(send_rows[0]))
    received = lax.all_to_all(outgoing, "pair", split_axis=0, concat_axis=0, tiled=True)
    shares = correlate(received, jnp.transpose(pair_slots), hours)
    stacked = stack_hours(shares, hours * hour_devices)
    stacked = stacked.reshape(COMPS * COMPS, pairs, LAGS)
    return jnp.transpose(stacked, (1, 0, 2))


def solution(mesh):
    return jax.shard_map(
        local,
        mesh=mesh,
        in_specs=(
            P("pair", "hour", None, None),
            P("pair", "hour", None),
            P("pair", "hour", None),
            P("pair", None, None),
            P("pair", None),
        ),
        out_specs=P("pair", None, None),
        check_vma=False,
    )
```

```python
import functools
import math

import jax
import jax.numpy as jnp
import ml_dtypes
import numpy as np
from jax import lax
from jax.experimental import pallas as pl
from jax.experimental.pallas import tpu as pltpu
from jax.sharding import PartitionSpec as P

NFFT = 1024
NFREQ = 512
LAGS = 256
COMPS = 3
WINDOWS = 2
PARTS = 2 * WINDOWS
SMOOTH_HALF = 11
EPS_WHITE = 1e-06
HALF_HOURS = 4
WHITEN_VMEM = 58 * 2**20
CORRELATE_VMEM = 24 * 2**20
SPREAD_VMEM = 8 * 2**20
F32 = jnp.float32
BF16 = jnp.bfloat16


def dft_table():
    turns = np.outer(np.arange(NFFT), np.arange(NFREQ)) % NFFT
    angles = turns.astype(np.float32) * np.float32(2.0 * math.pi / NFFT)
    angles = angles.astype(np.float64)
    table = np.concatenate([np.cos(angles), -np.sin(angles)], axis=1)
    return table.astype(np.float32).astype(ml_dtypes.bfloat16)


def band_table():
    index = np.arange(NFREQ)
    band = np.abs(index[:, None] - index[None, :]) <= SMOOTH_HALF
    return band.astype(ml_dtypes.bfloat16)


def lag_table():
    turns = np.outer(np.arange(NFREQ), np.arange(LAGS) - LAGS // 2) % NFFT
    angles = turns.astype(np.float32) * np.float32(2.0 * math.pi / NFFT)
    angles = angles.astype(np.float64)
    weights = np.where(np.arange(NFREQ) == 0, 0.5, 1.0)[:, None]
    table = np.concatenate([weights * np.cos(angles), -weights * np.sin(angles)], axis=0)
    scale = 1.0 / math.sqrt(WINDOWS * NFREQ)
    return (table.astype(np.float32).astype(ml_dtypes.bfloat16) * scale).astype(ml_dtypes.bfloat16)


def column(row, size):
    here = lax.broadcasted_iota(jnp.int32, (size, size), 0)
    there = lax.broadcasted_iota(jnp.int32, (size, size), 1)
    spread = jnp.where(here == there, jnp.broadcast_to(row, (size, size)).astype(F32), 0.0)
    return jnp.sum(spread, axis=1, keepdims=True).astype(jnp.int32)


def cut(panel, start):
    stations, raw = panel.shape
    reach = raw - 2048
    bit = (start & 2048) != 0
    moved = jnp.where(bit, panel[:, 2048:], panel[:, :reach])
    samples = jnp.concatenate([moved, panel[:, reach : NFFT + 2048]], axis=1)
    for size in (1024, 512, 256, 128):
        bit = (start & size) != 0
        keep = NFFT + size
        samples = jnp.where(bit, samples[:, size : size + keep], samples[:, :keep])
    place = lax.broadcasted_iota(jnp.int32, (stations, 128), 1) + (start & 127)
    inside = place & 127
    turned = [
        jnp.take_along_axis(samples[:, t : t + 128], inside, axis=1, mode="promise_in_bounds")
        for t in range(0, NFFT + 128, 128)
    ]
    beyond = place >= 128
    return jnp.concatenate([jnp.where(beyond, turned[t + 1], turned[t]) for t in range(NFFT // 128)], axis=1)


def whiten_kernel(
    raw_hbm, start_hbm, count_hbm, send_hbm, dft_hbm, band_hbm, out_hbm,
    raw_ref, start_ref, count_ref, send_ref, dft_ref, band_ref, seg_ref, spec_ref, white_ref, pick_ref, out_ref,
    small_sem, raw_sem, table_sem, out_sem,
):
    hours, _, stations, _ = raw_ref.shape
    capacity, owners = send_ref.shape
    rows = capacity * PARTS
    block = COMPS * WINDOWS * stations
    small_copies = [
        pltpu.make_async_copy(start_hbm, start_ref, small_sem.at[0]),
        pltpu.make_async_copy(count_hbm, count_ref, small_sem.at[1]),
        pltpu.make_async_copy(send_hbm, send_ref, small_sem.at[2]),
    ]
    raw_copies = [pltpu.make_async_copy(raw_hbm.at[h], raw_ref.at[h], raw_sem.at[h]) for h in range(hours)]
    dft_copy = pltpu.make_async_copy(dft_hbm, dft_ref, table_sem.at[0])
    band_copy = pltpu.make_async_copy(band_hbm, band_ref, table_sem.at[1])
    for copy in small_copies + raw_copies:
        copy.start()
    dft_copy.start()
    band_copy.start()
    for copy in small_copies:
        copy.wait()

    out_row = lax.broadcasted_iota(jnp.int32, (owners * rows, owners), 0)
    owner = lax.broadcasted_iota(jnp.int32, (owners * rows, owners), 1)
    spread = (out_row // rows == owner).astype(BF16)
    wanted = lax.dot_general(
        spread, send_ref[...].astype(F32).astype(BF16), (((1,), (1,)), ((), ())), preferred_element_type=F32
    )
    out_row = lax.broadcasted_iota(jnp.int32, (owners * rows, capacity), 0)
    place = lax.broadcasted_iota(jnp.int32, (owners * rows, capacity), 1)
    wanted = jnp.sum(jnp.where(out_row % rows // PARTS == place, wanted, 0.0), axis=1, keepdims=True).astype(jnp.int32)
    out_row = lax.broadcasted_iota(jnp.int32, (owners * rows, PARTS * stations), 0)
    white_row = lax.broadcasted_iota(jnp.int32, (owners * rows, PARTS * stations), 1)
    pick_ref[...] = (out_row % PARTS * stations + wanted == white_row).astype(BF16)

    time = lax.broadcasted_iota(jnp.int32, (stations, NFFT), 1)
    out_copies = []

    def cut_hour(h):
        raw_copies[h].wait()
        for w in range(WINDOWS):
            start = column(start_ref[h, w : w + 1, :], stations)
            count = column(count_ref[h, w : w + 1, :], stations)
            live = time < count
            share = count.astype(F32)
            for c in range(COMPS):
                piece = cut(raw_ref[h, c].astype(F32), start)
                piece = jnp.where(live, piece, 0.0)
                mean = jnp.sum(piece, axis=1, keepdims=True) / share
                row = h * block + (w * COMPS + c) * stations
                seg_ref[row : row + stations, :] = jnp.where(live, piece - mean, 0.0).astype(BF16)

    def send_hour(h):
        here = slice(h * block, (h + 1) * block)
        spec_ref[here, :] = jnp.dot(seg_ref[here, :], dft_ref[...], preferred_element_type=F32)
        amps = []
        for w in range(WINDOWS):
            total = jnp.zeros((stations, NFREQ), F32)
            for c in range(COMPS):
                row = h * block + (w * COMPS + c) * stations
                real = spec_ref[row : row + stations, :NFREQ]
                imag = spec_ref[row : row + stations, NFREQ:]
                total = total + jnp.sqrt(real * real + imag * imag)
            amps.append(total)
        amp = jnp.concatenate(amps, axis=0)
        size = WINDOWS * stations
        high = amp.astype(BF16)
        rest = amp - high.astype(F32)
        middle = rest.astype(BF16)
        low = (rest - middle.astype(F32)).astype(BF16)
        sums = jnp.dot(jnp.concatenate([high, middle, low], axis=0), band_ref[...], preferred_element_type=F32)
        smooth = (sums[:size] + sums[size : 2 * size] + sums[2 * size :]) / (3.0 * (2 * SMOOTH_HALF + 1))
        inverse = 1.0 / (smooth + EPS_WHITE)
        for c in range(COMPS):
            cols = slice(c * NFREQ, (c + 1) * NFREQ)
            for w in range(WINDOWS):
                factor = inverse[w * stations : (w + 1) * stations]
                row = h * block + (w * COMPS + c) * stations
                for r in range(2):
                    part = spec_ref[row : row + stations, r * NFREQ : (r + 1) * NFREQ] * factor
                    to = (2 * w + r) * stations
                    white_ref[h, to : to + stations, cols] = part.astype(BF16)
            picked = jnp.dot(pick_ref[...], white_ref[h, :, cols], preferred_element_type=F32).astype(BF16)
            out_ref[h, :, :, cols] = picked.reshape(owners, rows, NFREQ)
        copy = pltpu.make_async_copy(out_ref.at[h], out_hbm.at[:, pl.ds(h * rows, rows), :], out_sem.at[h])
        copy.start()
        out_copies.append(copy)

    cut_hour(0)
    dft_copy.wait()
    band_copy.wait()
    for h in range(hours):
        if h + 1 < hours:
            cut_hour(h + 1)
        send_hour(h)
    for copy in out_copies:
        copy.wait()


def share_of(device):
    return jnp.minimum(device, 2 * HALF_HOURS - 1 - device)


def correlate_kernel(recv_ref, slots_ref, lag_ref, *refs):
    out_refs, (pick_ref, side_ref, cross_ref, total_ref) = refs[:HALF_HOURS], refs[HALF_HOURS:]
    pairs = slots_ref.shape[1]
    owners, all_rows, _ = recv_ref.shape
    rows = all_rows // cross_ref.shape[0]
    half = NFREQ // 2

    arrived_row = lax.broadcasted_iota(jnp.int32, (pairs, owners * rows), 1)
    for side in range(2):
        first = column(slots_ref[side : side + 1, :], pairs) * PARTS
        for part in range(PARTS):
            row = (side * PARTS + part) * pairs
            pick_ref[row : row + pairs, :] = (first + part == arrived_row).astype(BF16)

    def select(h, n):
        for c in range(COMPS):
            col = c * NFREQ + n * half
            arrived = recv_ref[:, h * rows : (h + 1) * rows, col : col + half].reshape(owners * rows, half)
            side_ref[n, :, c * half : (c + 1) * half] = jnp.dot(pick_ref[...], arrived, preferred_element_type=F32)

    def cross(h, n):
        for k in range(0, pairs, 16):
            for f in range(0, half, 128):
                def load(side, part, comp):
                    row = (side * PARTS + part) * pairs + k
                    col = comp * half + f
                    return side_ref[n, row : row + 16, col : col + 128]
                left = [[load(0, part, comp) for comp in range(COMPS)] for part in range(PARTS)]
                right = [[load(1, part, comp) for comp in range(COMPS)] for part in range(PARTS)]
                for i in range(COMPS):
                    for j in range(COMPS):
                        real = left[0][i] * right[0][j] + left[2][i] * right[2][j]
                        real = real + (left[1][i] * right[1][j] + left[3][i] * right[3][j])
                        imag = left[1][i] * right[0][j] + left[3][i] * right[2][j]
                        imag = imag - (left[0][i] * right[1][j] + left[2][i] * right[3][j])
                        row = (COMPS * i + j) * pairs + k
                        col = n * half + f
                        cross_ref[h, row : row + 16, col : col + 128] = real.astype(BF16)
                        cross_ref[h, row : row + 16, NFREQ + col : NFREQ + col + 128] = imag.astype(BF16)

    def root(h):
        lagged = jnp.dot(cross_ref[h], lag_ref[...], preferred_element_type=F32)
        size = jnp.abs(lagged) + 0.01
        rooted = size * lax.rsqrt(size) - 0.1
        rooted = jnp.where(lagged < 0.0, -rooted, rooted)
        rooted = rooted.reshape(total_ref.shape)
        if h == 0:
            total_ref[...] = rooted
        else:
            total_ref[...] += rooted

    steps = [(h, n) for h in range(cross_ref.shape[0]) for n in range(2)]
    select(*steps[0])
    for now, later in zip(steps, steps[1:] + [None]):
        if later is not None:
            select(*later)
        cross(*now)
        if now[1] == 1:
            root(now[0])
    me = lax.axis_index("hour")
    for k, out_ref in enumerate(out_refs):
        out_ref[...] = total_ref[share_of(me ^ k)].astype(BF16)


def whiten(panels, starts, counts, send):
    hours, _, stations, raw = panels.shape
    capacity, owners = send.shape
    rows = capacity * PARTS
    width = COMPS * NFREQ
    block = WINDOWS * COMPS * stations
    hbm = pl.BlockSpec(memory_space=pltpu.HBM)
    return pl.pallas_call(
        whiten_kernel,
        in_specs=[hbm] * 6,
        out_specs=hbm,
        out_shape=jax.ShapeDtypeStruct((owners, hours * rows, width), BF16),
        scratch_shapes=[
            pltpu.VMEM(panels.shape, BF16),
            pltpu.VMEM(starts.shape, jnp.int32),
            pltpu.VMEM(counts.shape, jnp.int32),
            pltpu.VMEM(send.shape, jnp.int32),
            pltpu.VMEM((NFFT, 2 * NFREQ), BF16),
            pltpu.VMEM((NFREQ, NFREQ), BF16),
            pltpu.VMEM((hours * block, NFFT), BF16),
            pltpu.VMEM((hours * block, 2 * NFREQ), F32),
            pltpu.VMEM((hours, PARTS * stations, width), BF16),
            pltpu.VMEM((owners * rows, PARTS * stations), BF16),
            pltpu.VMEM((hours, owners, rows, width), BF16),
            pltpu.SemaphoreType.DMA((3,)),
            pltpu.SemaphoreType.DMA((hours,)),
            pltpu.SemaphoreType.DMA((2,)),
            pltpu.SemaphoreType.DMA((hours,)),
        ],
        compiler_params=pltpu.CompilerParams(vmem_limit_bytes=WHITEN_VMEM),
    )(panels, starts, counts, send, dft_table(), band_table())


def correlate(received, slots, hours):
    owners, all_rows, width = received.shape
    pairs = slots.shape[1]
    rows = all_rows // hours
    channels = COMPS * COMPS
    vmem = pl.BlockSpec(memory_space=pltpu.VMEM)
    share = (channels * pairs // HALF_HOURS, LAGS)
    return pl.pallas_call(
        correlate_kernel,
        in_specs=[vmem, vmem, vmem],
        out_specs=[vmem] * HALF_HOURS,
        out_shape=[jax.ShapeDtypeStruct(share, BF16)] * HALF_HOURS,
        scratch_shapes=[
            pltpu.VMEM((2 * PARTS * pairs, owners * rows), BF16),
            pltpu.VMEM((2, 2 * PARTS * pairs, width // 2), F32),
            pltpu.VMEM((hours, channels * pairs, 2 * NFREQ), BF16),
            pltpu.VMEM((HALF_HOURS,) + share, F32),
        ],
        compiler_params=pltpu.CompilerParams(vmem_limit_bytes=CORRELATE_VMEM),
    )(received, slots, lag_table())


def spread_kernel(*refs):
    part_refs, out_ref = refs[:-1], refs[-1]
    me = lax.axis_index("hour")
    for k, part_ref in enumerate(part_refs):
        out_ref[share_of(me ^ k)] = part_ref[...].astype(F32)


def swap(array, distance):
    return lax.ppermute(array, "hour", [(i, i ^ distance) for i in range(2 * HALF_HOURS)])


def stack_hours(shares, hours_all):
    mine = shares[0].astype(F32)
    for k in (2, 1, 3):
        mine = mine + swap(shares[k], k).astype(F32)
    mine = mine.astype(BF16)
    other = swap(mine, 2 * HALF_HOURS - 1)
    average = (mine.astype(F32) + other.astype(F32)) / hours_all
    size = jnp.abs(average) + 0.1
    stacked = (jnp.sign(average) * (size * size - 0.01)).astype(BF16)
    others = {k: swap(stacked, k) for k in (1, 2, 3)}
    parts = [stacked] + [others[k] for k in range(1, HALF_HOURS)]
    return pl.pallas_call(
        spread_kernel,
        out_shape=jax.ShapeDtypeStruct((HALF_HOURS,) + stacked.shape, F32),
        compiler_params=pltpu.CompilerParams(vmem_limit_bytes=SPREAD_VMEM),
        name="spread_result",
    )(*parts)


def local(raw_panels, window_start, valid_count, send_rows, pair_slots):
    hours = raw_panels.shape[1]
    pairs = pair_slots.shape[0]
    hour_devices = lax.axis_size("hour")
    panels = jnp.transpose(raw_panels, (1, 2, 0, 3))
    starts = jnp.transpose(window_start, (1, 2, 0))
    counts = jnp.transpose(valid_count, (1, 2, 0))
    outgoing = whiten(panels, starts, counts, jnp.transpose(send_rows[0]))
    received = lax.all_to_all(outgoing, "pair", split_axis=0, concat_axis=0, tiled=True)
    shares = correlate(received, jnp.transpose(pair_slots), hours)
    stacked = stack_hours(shares, hours * hour_devices)
    stacked = stacked.reshape(COMPS * COMPS, pairs, LAGS)
    return jnp.transpose(stacked, (1, 0, 2))


def solution(mesh):
    return jax.shard_map(
        local,
        mesh=mesh,
        in_specs=(
            P("pair", "hour", None, None),
            P("pair", "hour", None),
            P("pair", "hour", None),
            P("pair", None, None),
            P("pair", None),
        ),
        out_specs=P("pair", None, None),
        check_vma=False,
    )
```

```python
import functools
import math

import jax
import jax.numpy as jnp
import ml_dtypes
import numpy as np
from jax import lax
from jax.experimental import pallas as pl
from jax.experimental.pallas import tpu as pltpu
from jax.sharding import PartitionSpec as P

NFFT = 1024
NFREQ = 512
LAGS = 256
COMPS = 3
WINDOWS = 2
PARTS = 2 * WINDOWS
SMOOTH_HALF = 11
EPS_WHITE = 1e-06
HALF_HOURS = 4
WHITEN_VMEM = 58 * 2**20
CORRELATE_VMEM = 24 * 2**20
SPREAD_VMEM = 8 * 2**20
F32 = jnp.float32
BF16 = jnp.bfloat16


def dft_table():
    turns = np.outer(np.arange(NFFT), np.arange(NFREQ)) % NFFT
    angles = turns.astype(np.float32) * np.float32(2.0 * math.pi / NFFT)
    angles = angles.astype(np.float64)
    table = np.concatenate([np.cos(angles), -np.sin(angles)], axis=1)
    return table.astype(np.float32).astype(ml_dtypes.bfloat16)


def band_table():
    index = np.arange(NFREQ)
    band = np.abs(index[:, None] - index[None, :]) <= SMOOTH_HALF
    return band.astype(ml_dtypes.bfloat16)


def lag_table():
    turns = np.outer(np.arange(NFREQ), np.arange(LAGS) - LAGS // 2) % NFFT
    angles = turns.astype(np.float32) * np.float32(2.0 * math.pi / NFFT)
    angles = angles.astype(np.float64)
    weights = np.where(np.arange(NFREQ) == 0, 0.5, 1.0)[:, None]
    table = np.concatenate([weights * np.cos(angles), -weights * np.sin(angles)], axis=0)
    scale = 1.0 / math.sqrt(WINDOWS * NFREQ)
    return (table.astype(np.float32).astype(ml_dtypes.bfloat16) * scale).astype(ml_dtypes.bfloat16)


def column(row, size):
    here = lax.broadcasted_iota(jnp.int32, (size, size), 0)
    there = lax.broadcasted_iota(jnp.int32, (size, size), 1)
    spread = jnp.where(here == there, jnp.broadcast_to(row, (size, size)).astype(F32), 0.0)
    return jnp.sum(spread, axis=1, keepdims=True).astype(jnp.int32)


def cut(panel, start):
    stations, raw = panel.shape
    reach = raw - 2048
    bit = (start & 2048) != 0
    moved = jnp.where(bit, panel[:, 2048:], panel[:, :reach])
    samples = jnp.concatenate([moved, panel[:, reach : NFFT + 2048]], axis=1)
    for size in (1024, 512, 256, 128):
        bit = (start & size) != 0
        keep = NFFT + size
        samples = jnp.where(bit, samples[:, size : size + keep], samples[:, :keep])
    place = lax.broadcasted_iota(jnp.int32, (stations, 128), 1) + (start & 127)
    inside = place & 127
    turned = [
        jnp.take_along_axis(samples[:, t : t + 128], inside, axis=1, mode="promise_in_bounds")
        for t in range(0, NFFT + 128, 128)
    ]
    beyond = place >= 128
    return jnp.concatenate([jnp.where(beyond, turned[t + 1], turned[t]) for t in range(NFFT // 128)], axis=1)


def whiten_kernel(
    raw_hbm, start_hbm, count_hbm, send_hbm, slots_hbm, dft_hbm, band_hbm, out_hbm, pair_hbm,
    raw_ref, start_ref, count_ref, send_ref, dft_ref, band_ref, seg_ref, spec_ref, white_ref, pick_ref, out_ref,
    slots_ref, pair_ref, small_sem, raw_sem, table_sem, out_sem, pair_sem,
):
    hours, _, stations, _ = raw_ref.shape
    capacity, owners = send_ref.shape
    rows = capacity * PARTS
    block = COMPS * WINDOWS * stations
    small_copies = [
        pltpu.make_async_copy(start_hbm, start_ref, small_sem.at[0]),
        pltpu.make_async_copy(count_hbm, count_ref, small_sem.at[1]),
        pltpu.make_async_copy(send_hbm, send_ref, small_sem.at[2]),
        pltpu.make_async_copy(slots_hbm, slots_ref, small_sem.at[3]),
    ]
    raw_copies = [pltpu.make_async_copy(raw_hbm.at[h], raw_ref.at[h], raw_sem.at[h]) for h in range(hours)]
    dft_copy = pltpu.make_async_copy(dft_hbm, dft_ref, table_sem.at[0])
    band_copy = pltpu.make_async_copy(band_hbm, band_ref, table_sem.at[1])
    for copy in small_copies + raw_copies:
        copy.start()
    dft_copy.start()
    band_copy.start()
    for copy in small_copies:
        copy.wait()

    out_row = lax.broadcasted_iota(jnp.int32, (owners * rows, owners), 0)
    owner = lax.broadcasted_iota(jnp.int32, (owners * rows, owners), 1)
    spread = (out_row // rows == owner).astype(BF16)
    wanted = lax.dot_general(
        spread, send_ref[...].astype(F32).astype(BF16), (((1,), (1,)), ((), ())), preferred_element_type=F32
    )
    out_row = lax.broadcasted_iota(jnp.int32, (owners * rows, capacity), 0)
    place = lax.broadcasted_iota(jnp.int32, (owners * rows, capacity), 1)
    wanted = jnp.sum(jnp.where(out_row % rows // PARTS == place, wanted, 0.0), axis=1, keepdims=True).astype(jnp.int32)
    out_row = lax.broadcasted_iota(jnp.int32, (owners * rows, PARTS * stations), 0)
    white_row = lax.broadcasted_iota(jnp.int32, (owners * rows, PARTS * stations), 1)
    pick_ref[...] = (out_row % PARTS * stations + wanted == white_row).astype(BF16)

    pairs = slots_ref.shape[1]
    arrived_row = lax.broadcasted_iota(jnp.int32, (pairs, owners * rows), 1)
    for side in range(2):
        first = column(slots_ref[side : side + 1, :], pairs) * PARTS
        for part in range(PARTS):
            row = (side * PARTS + part) * pairs
            pair_ref[row : row + pairs, :] = (first + part == arrived_row).astype(BF16)

    pair_copy = pltpu.make_async_copy(pair_ref, pair_hbm, pair_sem)
    pair_copy.start()

    time = lax.broadcasted_iota(jnp.int32, (stations, NFFT), 1)
    out_copies = []

    def cut_hour(h):
        raw_copies[h].wait()
        for w in range(WINDOWS):
            start = column(start_ref[h, w : w + 1, :], stations)
            count = column(count_ref[h, w : w + 1, :], stations)
            live = time < count
            share = count.astype(F32)
            for c in range(COMPS):
                piece = cut(raw_ref[h, c].astype(F32), start)
                piece = jnp.where(live, piece, 0.0)
                mean = jnp.sum(piece, axis=1, keepdims=True) / share
                row = h * block + (w * COMPS + c) * stations
                seg_ref[row : row + stations, :] = jnp.where(live, piece - mean, 0.0).astype(BF16)

    def send_hour(h):
        here = slice(h * block, (h + 1) * block)
        spec_ref[here, :] = jnp.dot(seg_ref[here, :], dft_ref[...], preferred_element_type=F32)
        amps = []
        for w in range(WINDOWS):
            total = jnp.zeros((stations, NFREQ), F32)
            for c in range(COMPS):
                row = h * block + (w * COMPS + c) * stations
                real = spec_ref[row : row + stations, :NFREQ]
                imag = spec_ref[row : row + stations, NFREQ:]
                total = total + jnp.sqrt(real * real + imag * imag)
            amps.append(total)
        amp = jnp.concatenate(amps, axis=0)
        size = WINDOWS * stations
        high = amp.astype(BF16)
        rest = amp - high.astype(F32)
        middle = rest.astype(BF16)
        low = (rest - middle.astype(F32)).astype(BF16)
        sums = jnp.dot(jnp.concatenate([high, middle, low], axis=0), band_ref[...], preferred_element_type=F32)
        smooth = (sums[:size] + sums[size : 2 * size] + sums[2 * size :]) / (3.0 * (2 * SMOOTH_HALF + 1))
        inverse = 1.0 / (smooth + EPS_WHITE)
        for c in range(COMPS):
            cols = slice(c * NFREQ, (c + 1) * NFREQ)
            for w in range(WINDOWS):
                factor = inverse[w * stations : (w + 1) * stations]
                row = h * block + (w * COMPS + c) * stations
                for r in range(2):
                    part = spec_ref[row : row + stations, r * NFREQ : (r + 1) * NFREQ] * factor
                    to = (2 * w + r) * stations
                    white_ref[h, to : to + stations, cols] = part.astype(BF16)
            picked = jnp.dot(pick_ref[...], white_ref[h, :, cols], preferred_element_type=F32).astype(BF16)
            out_ref[h, :, :, cols] = picked.reshape(owners, rows, NFREQ)
        copy = pltpu.make_async_copy(out_ref.at[h], out_hbm.at[:, pl.ds(h * rows, rows), :], out_sem.at[h])
        copy.start()
        out_copies.append(copy)

    cut_hour(0)
    dft_copy.wait()
    band_copy.wait()
    for h in range(hours):
        if h + 1 < hours:
            cut_hour(h + 1)
        send_hour(h)
    for copy in out_copies:
        copy.wait()
    pair_copy.wait()


def share_of(device):
    return jnp.minimum(device, 2 * HALF_HOURS - 1 - device)


def correlate_kernel(recv_ref, pick_ref, lag_ref, *refs):
    out_refs, (side_ref, cross_ref, total_ref) = refs[:HALF_HOURS], refs[HALF_HOURS:]
    pairs = pick_ref.shape[0] // (2 * PARTS)
    owners, all_rows, _ = recv_ref.shape
    rows = all_rows // cross_ref.shape[0]
    half = NFREQ // 2

    def select(h, n):
        for c in range(COMPS):
            col = c * NFREQ + n * half
            arrived = recv_ref[:, h * rows : (h + 1) * rows, col : col + half].reshape(owners * rows, half)
            side_ref[n, :, c * half : (c + 1) * half] = jnp.dot(pick_ref[...], arrived, preferred_element_type=F32)

    def cross(h, n):
        for k in range(0, pairs, 16):
            for f in range(0, half, 128):
                def load(side, part, comp):
                    row = (side * PARTS + part) * pairs + k
                    col = comp * half + f
                    return side_ref[n, row : row + 16, col : col + 128]
                left = [[load(0, part, comp) for comp in range(COMPS)] for part in range(PARTS)]
                right = [[load(1, part, comp) for comp in range(COMPS)] for part in range(PARTS)]
                for i in range(COMPS):
                    for j in range(COMPS):
                        real = left[0][i] * right[0][j] + left[2][i] * right[2][j]
                        real = real + (left[1][i] * right[1][j] + left[3][i] * right[3][j])
                        imag = left[1][i] * right[0][j] + left[3][i] * right[2][j]
                        imag = imag - (left[0][i] * right[1][j] + left[2][i] * right[3][j])
                        row = (COMPS * i + j) * pairs + k
                        col = n * half + f
                        cross_ref[h, row : row + 16, col : col + 128] = real.astype(BF16)
                        cross_ref[h, row : row + 16, NFREQ + col : NFREQ + col + 128] = imag.astype(BF16)

    def root(h):
        lagged = jnp.dot(cross_ref[h], lag_ref[...], preferred_element_type=F32)
        size = jnp.abs(lagged) + 0.01
        rooted = size * lax.rsqrt(size) - 0.1
        rooted = jnp.where(lagged < 0.0, -rooted, rooted)
        rooted = rooted.reshape(total_ref.shape)
        if h == 0:
            total_ref[...] = rooted
        else:
            total_ref[...] += rooted

    steps = [(h, n) for h in range(cross_ref.shape[0]) for n in range(2)]
    select(*steps[0])
    for now, later in zip(steps, steps[1:] + [None]):
        if later is not None:
            select(*later)
        cross(*now)
        if now[1] == 1:
            root(now[0])
    me = lax.axis_index("hour")
    for k, out_ref in enumerate(out_refs):
        out_ref[...] = total_ref[share_of(me ^ k)].astype(BF16)


def whiten(panels, starts, counts, send, slots):
    hours, _, stations, raw = panels.shape
    capacity, owners = send.shape
    rows = capacity * PARTS
    width = COMPS * NFREQ
    block = WINDOWS * COMPS * stations
    pair_pick = (2 * PARTS * slots.shape[1], owners * rows)
    hbm = pl.BlockSpec(memory_space=pltpu.HBM)
    return pl.pallas_call(
        whiten_kernel,
        in_specs=[hbm] * 7,
        out_specs=[hbm, hbm],
        out_shape=[
            jax.ShapeDtypeStruct((owners, hours * rows, width), BF16),
            jax.ShapeDtypeStruct(pair_pick, BF16),
        ],
        scratch_shapes=[
            pltpu.VMEM(panels.shape, BF16),
            pltpu.VMEM(starts.shape, jnp.int32),
            pltpu.VMEM(counts.shape, jnp.int32),
            pltpu.VMEM(send.shape, jnp.int32),
            pltpu.VMEM((NFFT, 2 * NFREQ), BF16),
            pltpu.VMEM((NFREQ, NFREQ), BF16),
            pltpu.VMEM((hours * block, NFFT), BF16),
            pltpu.VMEM((hours * block, 2 * NFREQ), F32),
            pltpu.VMEM((hours, PARTS * stations, width), BF16),
            pltpu.VMEM((owners * rows, PARTS * stations), BF16),
            pltpu.VMEM((hours, owners, rows, width), BF16),
            pltpu.VMEM(slots.shape, jnp.int32),
            pltpu.VMEM(pair_pick, BF16),
            pltpu.SemaphoreType.DMA((4,)),
            pltpu.SemaphoreType.DMA((hours,)),
            pltpu.SemaphoreType.DMA((2,)),
            pltpu.SemaphoreType.DMA((hours,)),
            pltpu.SemaphoreType.DMA(()),
        ],
        compiler_params=pltpu.CompilerParams(vmem_limit_bytes=WHITEN_VMEM),
    )(panels, starts, counts, send, slots, dft_table(), band_table())


def correlate(received, pick, hours):
    owners, all_rows, width = received.shape
    pairs = pick.shape[0] // (2 * PARTS)
    rows = all_rows // hours
    channels = COMPS * COMPS
    vmem = pl.BlockSpec(memory_space=pltpu.VMEM)
    share = (channels * pairs // HALF_HOURS, LAGS)
    return pl.pallas_call(
        correlate_kernel,
        in_specs=[vmem, vmem, vmem],
        out_specs=[vmem] * HALF_HOURS,
        out_shape=[jax.ShapeDtypeStruct(share, BF16)] * HALF_HOURS,
        scratch_shapes=[
            pltpu.VMEM((2, 2 * PARTS * pairs, width // 2), F32),
            pltpu.VMEM((hours, channels * pairs, 2 * NFREQ), BF16),
            pltpu.VMEM((HALF_HOURS,) + share, F32),
        ],
        compiler_params=pltpu.CompilerParams(vmem_limit_bytes=CORRELATE_VMEM),
    )(received, pick, lag_table())


def spread_kernel(*refs):
    part_refs, out_ref = refs[:-1], refs[-1]
    me = lax.axis_index("hour")
    for k, part_ref in enumerate(part_refs):
        out_ref[share_of(me ^ k)] = part_ref[...].astype(F32)


def swap(array, distance):
    return lax.ppermute(array, "hour", [(i, i ^ distance) for i in range(2 * HALF_HOURS)])


def stack_hours(shares, hours_all):
    mine = shares[0].astype(F32)
    for k in (2, 1, 3):
        mine = mine + swap(shares[k], k).astype(F32)
    mine = mine.astype(BF16)
    other = swap(mine, 2 * HALF_HOURS - 1)
    average = (mine.astype(F32) + other.astype(F32)) / hours_all
    size = jnp.abs(average) + 0.1
    stacked = (jnp.sign(average) * (size * size - 0.01)).astype(BF16)
    others = {k: swap(stacked, k) for k in (1, 2, 3)}
    parts = [stacked] + [others[k] for k in range(1, HALF_HOURS)]
    return pl.pallas_call(
        spread_kernel,
        out_shape=jax.ShapeDtypeStruct((HALF_HOURS,) + stacked.shape, F32),
        compiler_params=pltpu.CompilerParams(vmem_limit_bytes=SPREAD_VMEM),
        name="spread_result",
    )(*parts)


def local(raw_panels, window_start, valid_count, send_rows, pair_slots):
    hours = raw_panels.shape[1]
    pairs = pair_slots.shape[0]
    hour_devices = lax.axis_size("hour")
    panels = jnp.transpose(raw_panels, (1, 2, 0, 3))
    starts = jnp.transpose(window_start, (1, 2, 0))
    counts = jnp.transpose(valid_count, (1, 2, 0))
    outgoing, pick = whiten(panels, starts, counts, jnp.transpose(send_rows[0]), jnp.transpose(pair_slots))
    received = lax.all_to_all(outgoing, "pair", split_axis=0, concat_axis=0, tiled=True)
    shares = correlate(received, pick, hours)
    stacked = stack_hours(shares, hours * hour_devices)
    stacked = stacked.reshape(COMPS * COMPS, pairs, LAGS)
    return jnp.transpose(stacked, (1, 0, 2))


def solution(mesh):
    return jax.shard_map(
        local,
        mesh=mesh,
        in_specs=(
            P("pair", "hour", None, None),
            P("pair", "hour", None),
            P("pair", "hour", None),
            P("pair", None, None),
            P("pair", None),
        ),
        out_specs=P("pair", None, None),
        check_vma=False,
    )
```

```python
import functools
import math

import jax
import jax.numpy as jnp
import ml_dtypes
import numpy as np
from jax import lax
from jax.experimental import pallas as pl
from jax.experimental.pallas import tpu as pltpu
from jax.sharding import PartitionSpec as P

NFFT = 1024
NFREQ = 512
LAGS = 256
COMPS = 3
WINDOWS = 2
PARTS = 2 * WINDOWS
SMOOTH_HALF = 11
EPS_WHITE = 1e-06
HALF_HOURS = 4
WHITEN_VMEM = 58 * 2**20
CORRELATE_VMEM = 24 * 2**20
SPREAD_VMEM = 8 * 2**20
F32 = jnp.float32
BF16 = jnp.bfloat16


def dft_table():
    turns = np.outer(np.arange(NFFT), np.arange(NFREQ)) % NFFT
    angles = turns.astype(np.float32) * np.float32(2.0 * math.pi / NFFT)
    angles = angles.astype(np.float64)
    table = np.concatenate([np.cos(angles), -np.sin(angles)], axis=1)
    return table.astype(np.float32).astype(ml_dtypes.bfloat16)


def band_table():
    index = np.arange(NFREQ)
    band = np.abs(index[:, None] - index[None, :]) <= SMOOTH_HALF
    return band.astype(ml_dtypes.bfloat16)


def lag_table():
    turns = np.outer(np.arange(NFREQ), np.arange(LAGS) - LAGS // 2) % NFFT
    angles = turns.astype(np.float32) * np.float32(2.0 * math.pi / NFFT)
    angles = angles.astype(np.float64)
    weights = np.where(np.arange(NFREQ) == 0, 0.5, 1.0)[:, None]
    table = np.concatenate([weights * np.cos(angles), -weights * np.sin(angles)], axis=0)
    scale = 1.0 / math.sqrt(WINDOWS * NFREQ)
    return (table.astype(np.float32).astype(ml_dtypes.bfloat16) * scale).astype(ml_dtypes.bfloat16)


def column(row, size):
    here = lax.broadcasted_iota(jnp.int32, (size, size), 0)
    there = lax.broadcasted_iota(jnp.int32, (size, size), 1)
    spread = jnp.where(here == there, jnp.broadcast_to(row, (size, size)).astype(F32), 0.0)
    return jnp.sum(spread, axis=1, keepdims=True).astype(jnp.int32)


def cut(panel, start):
    stations, raw = panel.shape
    reach = raw - 2048
    bit = (start & 2048) != 0
    moved = jnp.where(bit, panel[:, 2048:], panel[:, :reach])
    samples = jnp.concatenate([moved, panel[:, reach : NFFT + 2048]], axis=1)
    for size in (1024, 512, 256, 128):
        bit = (start & size) != 0
        keep = NFFT + size
        samples = jnp.where(bit, samples[:, size : size + keep], samples[:, :keep])
    place = lax.broadcasted_iota(jnp.int32, (stations, 128), 1) + (start & 127)
    inside = place & 127
    turned = [
        jnp.take_along_axis(samples[:, t : t + 128], inside, axis=1, mode="promise_in_bounds")
        for t in range(0, NFFT + 128, 128)
    ]
    beyond = place >= 128
    return jnp.concatenate([jnp.where(beyond, turned[t + 1], turned[t]) for t in range(NFFT // 128)], axis=1)


def whiten_kernel(
    raw_hbm, start_hbm, count_hbm, send_hbm, slots_hbm, dft_hbm, band_hbm, out_hbm, pair_hbm,
    raw_ref, start_ref, count_ref, send_ref, dft_ref, band_ref, seg_ref, spec_ref, white_ref, pick_ref, out_ref,
    slots_ref, pair_ref, small_sem, raw_sem, table_sem, out_sem, pair_sem,
):
    hours, _, stations, _ = raw_ref.shape
    capacity, owners = send_ref.shape
    rows = capacity * PARTS
    block = COMPS * WINDOWS * stations
    small_copies = [
        pltpu.make_async_copy(start_hbm, start_ref, small_sem.at[0]),
        pltpu.make_async_copy(count_hbm, count_ref, small_sem.at[1]),
        pltpu.make_async_copy(send_hbm, send_ref, small_sem.at[2]),
        pltpu.make_async_copy(slots_hbm, slots_ref, small_sem.at[3]),
    ]
    raw_copies = [pltpu.make_async_copy(raw_hbm.at[h], raw_ref.at[h], raw_sem.at[h]) for h in range(hours)]
    dft_copy = pltpu.make_async_copy(dft_hbm, dft_ref, table_sem.at[0])
    band_copy = pltpu.make_async_copy(band_hbm, band_ref, table_sem.at[1])
    for copy in small_copies + raw_copies:
        copy.start()
    dft_copy.start()
    band_copy.start()
    for copy in small_copies:
        copy.wait()

    out_row = lax.broadcasted_iota(jnp.int32, (owners * rows, owners), 0)
    owner = lax.broadcasted_iota(jnp.int32, (owners * rows, owners), 1)
    spread = (out_row // rows == owner).astype(BF16)
    wanted = lax.dot_general(
        spread, send_ref[...].astype(F32).astype(BF16), (((1,), (1,)), ((), ())), preferred_element_type=F32
    )
    out_row = lax.broadcasted_iota(jnp.int32, (owners * rows, capacity), 0)
    place = lax.broadcasted_iota(jnp.int32, (owners * rows, capacity), 1)
    wanted = jnp.sum(jnp.where(out_row % rows // PARTS == place, wanted, 0.0), axis=1, keepdims=True).astype(jnp.int32)
    out_row = lax.broadcasted_iota(jnp.int32, (owners * rows, PARTS * stations), 0)
    white_row = lax.broadcasted_iota(jnp.int32, (owners * rows, PARTS * stations), 1)
    pick_ref[...] = (out_row % PARTS * stations + wanted == white_row).astype(BF16)

    pairs = slots_ref.shape[1]
    arrived_row = lax.broadcasted_iota(jnp.int32, (pairs, owners * rows), 1)
    for side in range(2):
        first = column(slots_ref[side : side + 1, :], pairs) * PARTS
        for part in range(PARTS):
            row = (side * PARTS + part) * pairs
            pair_ref[row : row + pairs, :] = (first + part == arrived_row).astype(BF16)

    pair_copy = pltpu.make_async_copy(pair_ref, pair_hbm, pair_sem)
    pair_copy.start()

    time = lax.broadcasted_iota(jnp.int32, (stations, NFFT), 1)
    out_copies = []

    def cut_hour(h):
        raw_copies[h].wait()
        for w in range(WINDOWS):
            start = column(start_ref[h, w : w + 1, :], stations)
            count = column(count_ref[h, w : w + 1, :], stations)
            live = time < count
            share = count.astype(F32)
            for c in range(COMPS):
                piece = cut(raw_ref[h, c].astype(F32), start)
                piece = jnp.where(live, piece, 0.0)
                mean = jnp.sum(piece, axis=1, keepdims=True) / share
                row = h * block + (w * COMPS + c) * stations
                seg_ref[row : row + stations, :] = jnp.where(live, piece - mean, 0.0).astype(BF16)

    def send_hour(h):
        here = slice(h * block, (h + 1) * block)
        spec_ref[here, :] = jnp.dot(seg_ref[here, :], dft_ref[...], preferred_element_type=F32)
        amps = []
        for w in range(WINDOWS):
            total = jnp.zeros((stations, NFREQ), F32)
            for c in range(COMPS):
                row = h * block + (w * COMPS + c) * stations
                real = spec_ref[row : row + stations, :NFREQ]
                imag = spec_ref[row : row + stations, NFREQ:]
                total = total + jnp.sqrt(real * real + imag * imag)
            amps.append(total)
        amp = jnp.concatenate(amps, axis=0)
        size = WINDOWS * stations
        high = amp.astype(BF16)
        rest = amp - high.astype(F32)
        middle = rest.astype(BF16)
        low = (rest - middle.astype(F32)).astype(BF16)
        sums = jnp.dot(jnp.concatenate([high, middle, low], axis=0), band_ref[...], preferred_element_type=F32)
        smooth = (sums[:size] + sums[size : 2 * size] + sums[2 * size :]) / (3.0 * (2 * SMOOTH_HALF + 1))
        inverse = 1.0 / (smooth + EPS_WHITE)
        for c in range(COMPS):
            cols = slice(c * NFREQ, (c + 1) * NFREQ)
            for w in range(WINDOWS):
                factor = inverse[w * stations : (w + 1) * stations]
                row = h * block + (w * COMPS + c) * stations
                for r in range(2):
                    part = spec_ref[row : row + stations, r * NFREQ : (r + 1) * NFREQ] * factor
                    to = (2 * w + r) * stations
                    white_ref[h, to : to + stations, cols] = part.astype(BF16)
            picked = jnp.dot(pick_ref[...], white_ref[h, :, cols], preferred_element_type=F32).astype(BF16)
            out_ref[h, :, :, cols] = picked.reshape(owners, rows, NFREQ)
        copy = pltpu.make_async_copy(out_ref.at[h], out_hbm.at[:, pl.ds(h * rows, rows), :], out_sem.at[h])
        copy.start()
        out_copies.append(copy)

    cut_hour(0)
    dft_copy.wait()
    band_copy.wait()
    for h in range(hours):
        if h + 1 < hours:
            cut_hour(h + 1)
        send_hour(h)
    for copy in out_copies:
        copy.wait()
    pair_copy.wait()


def share_of(device):
    return jnp.minimum(device, 2 * HALF_HOURS - 1 - device)


def correlate_kernel(recv_ref, pick_ref, lag_ref, *refs):
    out_refs, (side_ref, cross_ref, total_ref) = refs[:HALF_HOURS], refs[HALF_HOURS:]
    pairs = pick_ref.shape[0] // (2 * PARTS)
    owners, all_rows, _ = recv_ref.shape
    rows = all_rows // cross_ref.shape[0]
    half = NFREQ // 2

    def select(h, n):
        for c in range(COMPS):
            col = c * NFREQ + n * half
            arrived = recv_ref[:, h * rows : (h + 1) * rows, col : col + half].reshape(owners * rows, half)
            side_ref[n, :, c * half : (c + 1) * half] = jnp.dot(pick_ref[...], arrived, preferred_element_type=F32)

    def cross(h, n):
        for k in range(0, pairs, 16):
            for f in range(0, half, 128):
                def load(side, part, comp):
                    row = (side * PARTS + part) * pairs + k
                    col = comp * half + f
                    return side_ref[n, row : row + 16, col : col + 128]
                left = [[load(0, part, comp) for comp in range(COMPS)] for part in range(PARTS)]
                right = [[load(1, part, comp) for comp in range(COMPS)] for part in range(PARTS)]
                for i in range(COMPS):
                    for j in range(COMPS):
                        real = left[0][i] * right[0][j] + left[2][i] * right[2][j]
                        real = real + (left[1][i] * right[1][j] + left[3][i] * right[3][j])
                        imag = left[1][i] * right[0][j] + left[3][i] * right[2][j]
                        imag = imag - (left[0][i] * right[1][j] + left[2][i] * right[3][j])
                        row = (COMPS * i + j) * pairs + k
                        col = n * half + f
                        cross_ref[h, row : row + 16, col : col + 128] = real.astype(BF16)
                        cross_ref[h, row : row + 16, NFREQ + col : NFREQ + col + 128] = imag.astype(BF16)

    def root(h):
        lagged = jnp.dot(cross_ref[h], lag_ref[...], preferred_element_type=F32)
        size = jnp.abs(lagged) + 0.01
        rooted = size * lax.rsqrt(size) - 0.1
        rooted = jnp.where(lagged < 0.0, -rooted, rooted)
        rooted = rooted.reshape(total_ref.shape)
        if h == 0:
            total_ref[...] = rooted
        else:
            total_ref[...] += rooted

    steps = [(h, n) for h in range(cross_ref.shape[0]) for n in range(2)]
    select(*steps[0])
    for now, later in zip(steps, steps[1:] + [None]):
        if later is not None:
            select(*later)
        cross(*now)
        if now[1] == 1:
            root(now[0])
    me = lax.axis_index("hour")
    for k, out_ref in enumerate(out_refs):
        out_ref[...] = total_ref[share_of(me ^ k)].astype(BF16)


def whiten(panels, starts, counts, send, slots):
    hours, _, stations, raw = panels.shape
    capacity, owners = send.shape
    rows = capacity * PARTS
    width = COMPS * NFREQ
    block = WINDOWS * COMPS * stations
    pair_pick = (2 * PARTS * slots.shape[1], owners * rows)
    hbm = pl.BlockSpec(memory_space=pltpu.HBM)
    return pl.pallas_call(
        whiten_kernel,
        in_specs=[hbm] * 7,
        out_specs=[hbm, hbm],
        out_shape=[
            jax.ShapeDtypeStruct((owners, hours * rows, width), BF16),
            jax.ShapeDtypeStruct(pair_pick, BF16),
        ],
        scratch_shapes=[
            pltpu.VMEM(panels.shape, BF16),
            pltpu.VMEM(starts.shape, jnp.int32),
            pltpu.VMEM(counts.shape, jnp.int32),
            pltpu.VMEM(send.shape, jnp.int32),
            pltpu.VMEM((NFFT, 2 * NFREQ), BF16),
            pltpu.VMEM((NFREQ, NFREQ), BF16),
            pltpu.VMEM((hours * block, NFFT), BF16),
            pltpu.VMEM((hours * block, 2 * NFREQ), F32),
            pltpu.VMEM((hours, PARTS * stations, width), BF16),
            pltpu.VMEM((owners * rows, PARTS * stations), BF16),
            pltpu.VMEM((hours, owners, rows, width), BF16),
            pltpu.VMEM(slots.shape, jnp.int32),
            pltpu.VMEM(pair_pick, BF16),
            pltpu.SemaphoreType.DMA((4,)),
            pltpu.SemaphoreType.DMA((hours,)),
            pltpu.SemaphoreType.DMA((2,)),
            pltpu.SemaphoreType.DMA((hours,)),
            pltpu.SemaphoreType.DMA(()),
        ],
        compiler_params=pltpu.CompilerParams(vmem_limit_bytes=WHITEN_VMEM),
    )(panels, starts, counts, send, slots, dft_table(), band_table())


def correlate(received, pick, hours):
    owners, all_rows, width = received.shape
    pairs = pick.shape[0] // (2 * PARTS)
    rows = all_rows // hours
    channels = COMPS * COMPS
    vmem = pl.BlockSpec(memory_space=pltpu.VMEM)
    share = (channels * pairs // HALF_HOURS, LAGS)
    return pl.pallas_call(
        correlate_kernel,
        in_specs=[vmem, vmem, vmem],
        out_specs=[vmem] * HALF_HOURS,
        out_shape=[jax.ShapeDtypeStruct(share, BF16)] * HALF_HOURS,
        scratch_shapes=[
            pltpu.VMEM((2, 2 * PARTS * pairs, width // 2), F32),
            pltpu.VMEM((hours, channels * pairs, 2 * NFREQ), BF16),
            pltpu.VMEM((HALF_HOURS,) + share, F32),
        ],
        compiler_params=pltpu.CompilerParams(vmem_limit_bytes=CORRELATE_VMEM),
    )(received, pick, lag_table())


def spread_kernel(*refs):
    part_refs, out_ref = refs[:-1], refs[-1]
    me = lax.axis_index("hour")
    for k, part_ref in enumerate(part_refs):
        out_ref[share_of(me ^ k)] = part_ref[...].astype(F32)


def swap(array, distance):
    return lax.ppermute(array, "hour", [(i, i ^ distance) for i in range(2 * HALF_HOURS)])


def stack_hours(shares, hours_all):
    mine = shares[0].astype(F32)
    for k in (2, 1, 3):
        mine = mine + swap(shares[k], k).astype(F32)
    mine = mine.astype(BF16)
    other = swap(mine, 2 * HALF_HOURS - 1)
    average = (mine.astype(F32) + other.astype(F32)) / hours_all
    size = jnp.abs(average) + 0.1
    stacked = (jnp.sign(average) * (size * size - 0.01)).astype(BF16)
    others = {k: swap(stacked, k) for k in (1, 3, 2)}
    parts = [stacked] + [others[k] for k in range(1, HALF_HOURS)]
    return pl.pallas_call(
        spread_kernel,
        out_shape=jax.ShapeDtypeStruct((HALF_HOURS,) + stacked.shape, F32),
        compiler_params=pltpu.CompilerParams(vmem_limit_bytes=SPREAD_VMEM),
        name="spread_result",
    )(*parts)


def local(raw_panels, window_start, valid_count, send_rows, pair_slots):
    hours = raw_panels.shape[1]
    pairs = pair_slots.shape[0]
    hour_devices = lax.axis_size("hour")
    panels = jnp.transpose(raw_panels, (1, 2, 0, 3))
    starts = jnp.transpose(window_start, (1, 2, 0))
    counts = jnp.transpose(valid_count, (1, 2, 0))
    outgoing, pick = whiten(panels, starts, counts, jnp.transpose(send_rows[0]), jnp.transpose(pair_slots))
    received = lax.all_to_all(outgoing, "pair", split_axis=0, concat_axis=0, tiled=True)
    shares = correlate(received, pick, hours)
    stacked = stack_hours(shares, hours * hour_devices)
    stacked = stacked.reshape(COMPS * COMPS, pairs, LAGS)
    return jnp.transpose(stacked, (1, 0, 2))


def solution(mesh):
    return jax.shard_map(
        local,
        mesh=mesh,
        in_specs=(
            P("pair", "hour", None, None),
            P("pair", "hour", None),
            P("pair", "hour", None),
            P("pair", None, None),
            P("pair", None),
        ),
        out_specs=P("pair", None, None),
        check_vma=False,
    )
```
